32 devices in a mesh: groups: 2 (over y), wide: 8 (over z, x), narrow: 2 (over core).
Axes of the slice: x: 2, y: 2, z: 4, core: 2. Of those that a mesh axis runs over, the one named last changes fastest.
Arguments:
- act_rows: bfloat16 [96, 7168], P(('groups', 'wide'), 'narrow'), parts along dimension 0, may hold values from -6 to 6
- routes: int32 [96, 3], P(('groups', 'wide')), parts along dimension 0, may hold values from 0 to 47, as said below
- route_weights: float32 [96, 3], P(('groups', 'wide')), parts along dimension 0, may hold values from 0.2 to 1
- owners: int32 [4], replicated, may hold values from 0 to 3, each once
- w_gate: bfloat16 [7168, 20480], P('narrow', 'wide'), may hold values from -0.0625 to 0.0625
- w_up: bfloat16 [7168, 20480], P('narrow', 'wide'), may hold values from -0.0625 to 0.0625
- w_down: bfloat16 [20480, 7168], P('wide', 'narrow'), may hold values from -0.078125 to 0.078125
- queries: bfloat16 [64, 64, 256], P(('groups', 'wide'), 'narrow'), parts along dimension 0, may hold values from -192 to 192
- new_keys: bfloat16 [64, 256], P(('groups', 'wide')), parts along dimension 0, may hold values from -6 to 6
- new_values: bfloat16 [64, 256], P(('groups', 'wide')), parts along dimension 0, may hold values from -6 to 6
- key_cache: bfloat16 [64, 256, 256], P(('groups', 'wide')), parts along dimension 0, may hold values from -6 to 6
- value_cache: bfloat16 [64, 256, 256], P(('groups', 'wide')), parts along dimension 0, may hold values from -6 to 6
- lengths: int32 [64], P(('groups', 'wide')), parts along dimension 0, may hold values from 1 to 256, as said below
Outputs:
- ffn_out: bfloat16 [96, 7168], P(('groups', 'wide'), 'narrow'), parts along dimension 0
- context: bfloat16 [64, 16384], P(('groups', 'wide'), 'narrow'), parts along dimension 0
The draws below stay inside these ranges and needn't reach their ends.
There are 2 independent parts, one for each index of `groups`. The reference program is written for one: setup_inputs(seed, part) draws one part's arguments, and reference() takes and returns one part's arrays. A program takes and returns all parts, laid end to end along the dimension named above; an argument that names none is the same for every part. Nothing has to cross between parts.
Inputs may be any that keep to these rules, and one draw needn't show every extreme that they name: `routes`: each token names 3 different experts, at most one of them below 4. Among the 6 tokens of one aligned block at most 2 name any one expert below 4; every expert below 4 is named in every block, and one of them is named by exactly 2 tokens of every block. `lengths`: some request of every part has 256.
All inputs are finite; a program needn't handle non-finite values.
Results may differ from the reference program's by a relative error of at most 0.0075.
Values may be sent and summed in bfloat16 or wider, within the bound.
No kernel may reach another device: no remote copies, remote signals or barrier semaphores. Data moves between devices by JAX's collectives and lax.ppermute only.
A program may use at most 128 MiB of HBM per device.

```python
import jax
import jax.numpy as jnp
from jax import lax

D = 7168
FF = 5120
E_ALL = 48
TOP = 3
HEADS = 64
HEAD_DIM = 256
EXPERTS = 4
TOK_DEV = 6
MAXLEN = 256
TOKENS = 48
REQUESTS = 32
CAP = 2
GROUP = 2
SHARD_HID = 2560


def shared_keys(key):
    base_keys = jax.random.normal(jax.random.fold_in(key, 5), (REQUESTS, HEAD_DIM), jnp.float32)
    return jnp.clip(base_keys, -6.0, 6.0)


def draw_new_keys(key, part):
    shared = shared_keys(key)
    return shared.astype(jnp.bfloat16)


def draw_key_cache(key, part):
    key = jax.random.fold_in(key, 12)
    cache_vals = jnp.clip(jax.random.normal(key, (REQUESTS, MAXLEN, HEAD_DIM), jnp.float32), -6.0, 6.0)
    return cache_vals.astype(jnp.bfloat16)


def draw_queries(key, part):
    shared = shared_keys(key)
    key = jax.random.fold_in(key, 13)
    query_vals = jax.random.normal(key, (REQUESTS, HEADS, HEAD_DIM), jnp.float32)
    query_vals = jnp.clip(query_vals + 3.0 * shared[:, None, :] * HEAD_DIM ** (-0.5), -6.0, 6.0)
    return query_vals.astype(jnp.bfloat16)


def draw_routes(key, part):
    key = jax.random.fold_in(key, 14)
    subkeys = jax.random.split(key, 6)
    blocks = TOKENS // TOK_DEV
    others = E_ALL - EXPERTS
    hot_expert = jax.random.randint(subkeys[0], (), 0, EXPERTS)
    counts = jax.random.randint(subkeys[1], (blocks, EXPERTS), 1, CAP // 2 + 1)
    counts = jnp.where(jnp.arange(EXPERTS)[None, :] == hot_expert, CAP, counts)
    starts = jnp.cumsum(counts, axis=1) - counts
    shuffle = jax.vmap(lambda sub: jax.random.permutation(sub, TOK_DEV))(jax.random.split(subkeys[2], blocks))
    places = jnp.arange(TOK_DEV)[None, :, None]
    inside = (places >= starts[:, None, :]) & (places < (starts + counts)[:, None, :])
    at_place = jnp.sum(jnp.where(inside, jnp.arange(EXPERTS)[None, None, :] + 1, 0), axis=2) - 1
    chosen = jnp.zeros((blocks, TOK_DEV), jnp.int32).at[jnp.arange(blocks)[:, None], shuffle].set(at_place)
    first_other = jax.random.randint(subkeys[3], (blocks, TOK_DEV), 0, others)
    stride = jax.random.randint(subkeys[4], (blocks, TOK_DEV), 1, (others - 1) // (TOP - 1) + 1)
    column = jnp.arange(TOP)[None, None, :]
    outside = EXPERTS + (first_other[..., None] + column * stride[..., None]) % others
    window_slot = jax.random.randint(subkeys[5], (blocks, TOK_DEV), 0, TOP)
    use_window = (column == window_slot[..., None]) & (chosen[..., None] >= 0)
    routes = jnp.where(use_window, chosen[..., None], outside)
    return routes.reshape(TOKENS, TOP).astype(jnp.int32)


def draw_lengths(key, part):
    key = jax.random.fold_in(key, 15)
    subkeys = jax.random.split(key, 2)
    lengths = jax.random.randint(subkeys[0], (REQUESTS,), 1, MAXLEN + 1)
    full_index = jax.random.randint(subkeys[1], (), 0, REQUESTS)
    return jnp.where(jnp.arange(REQUESTS) == full_index, MAXLEN, lengths).astype(jnp.int32)


def block_levels(rng, shape, cuts, low, top_value):
    loudness, own = 1.0, jax.random.fold_in(rng, 6)
    for dim, blocks in cuts:
        steps = jnp.exp(jax.random.uniform(jax.random.fold_in(own, dim), (blocks,), jnp.float32, low / len(cuts), top_value / len(cuts)))
        loudness = loudness * jnp.repeat(steps, shape[dim] // blocks).reshape([-1 if axis == dim else 1 for axis in range(len(shape))])
    return loudness


def bell_draw(own_key, extent, scale, limit, pieces=(), kind=jnp.bfloat16):
    entries = scale * jax.random.normal(own_key, extent, jnp.float32)
    if pieces:
        entries = entries * block_levels(own_key, extent, pieces, -0.22, 0.18)
    return jnp.clip(entries, -limit, limit).astype(kind)


def setup_inputs(seed: int = 0, part: int = 0) -> dict:
    keys = jax.random.split(jax.random.key(seed), 14)
    part_splits = jax.random.split(jax.random.fold_in(keys[13], part), 14)
    act_rows = bell_draw(part_splits[0], (TOKENS, D), 1.0, 6.0, ((0, 8), (1, 2)))
    routes = draw_routes(jax.random.fold_in(jax.random.fold_in(keys[13], part), 71), part)
    route_weights = jnp.clip(0.2 + 0.8 * jax.random.uniform(part_splits[2], (TOKENS, TOP), jnp.float32) ** block_levels(part_splits[2], (TOKENS, TOP), ((0, 8),), -0.2, 0.2), 0.2, 1.0)
    owners = jax.random.permutation(keys[3], EXPERTS).astype(jnp.int32)
    w_gate = bell_draw(keys[4], (D, EXPERTS * FF), D ** -0.5, 0.0625, ((0, 2), (1, 8)))
    w_up = bell_draw(keys[5], (D, EXPERTS * FF), D ** -0.5, 0.0625, ((0, 2), (1, 8)))
    w_down = bell_draw(keys[6], (EXPERTS * FF, D), FF ** -0.5, 0.078125, ((0, 8), (1, 2)))
    queries = draw_queries(jax.random.fold_in(jax.random.fold_in(keys[13], part), 71), part)
    new_keys = draw_new_keys(jax.random.fold_in(jax.random.fold_in(keys[13], part), 71), part)
    new_values = bell_draw(part_splits[9], (REQUESTS, HEAD_DIM), 1.0, 6.0, ((0, 8),))
    key_cache = draw_key_cache(jax.random.fold_in(jax.random.fold_in(keys[13], part), 71), part)
    value_cache = bell_draw(part_splits[11], (REQUESTS, MAXLEN, HEAD_DIM), 1.0, 6.0, ((0, 8),))
    lengths = draw_lengths(jax.random.fold_in(jax.random.fold_in(keys[13], part), 71), part)
    return {"act_rows": act_rows, "routes": routes, "route_weights": route_weights, "owners": owners, "w_gate": w_gate, "w_up": w_up, "w_down": w_down, "queries": queries, "new_keys": new_keys, "new_values": new_values, "key_cache": key_cache, "value_cache": value_cache, "lengths": lengths}


def attend(queries, new_keys, new_values, key_cache, value_cache, lengths):
    scaling = HEAD_DIM ** -0.5
    cached = jnp.einsum("rhd,rpd->rhp", queries.astype(jnp.float32), key_cache.astype(jnp.float32)) * scaling
    own_score = jnp.einsum("rhd,rd->rh", queries.astype(jnp.float32), new_keys.astype(jnp.float32)) * scaling
    places = lax.broadcasted_iota(jnp.int32, cached.shape, 2)
    cached = jnp.where(places < lengths[:, None, None], cached, -jnp.inf)
    row_max = jnp.maximum(jnp.max(cached, axis=2), own_score)
    cached_exp = jnp.exp(cached - row_max[:, :, None])
    own_exp = jnp.exp(own_score - row_max)
    denominator = jnp.sum(cached_exp, axis=2) + own_exp
    cached_prob = (cached_exp / denominator[:, :, None]).astype(jnp.bfloat16)
    own_prob = (own_exp / denominator).astype(jnp.bfloat16)
    mixture = jnp.einsum("rhp,rpd->rhd", cached_prob.astype(jnp.float32), value_cache.astype(jnp.float32))
    mixture = mixture + own_prob.astype(jnp.float32)[:, :, None] * new_values.astype(jnp.float32)[:, None, :]
    return mixture.astype(jnp.bfloat16).reshape(mixture.shape[0], HEADS * HEAD_DIM)


def expert_rows(row_block, gate_cols, up_cols, down_rows):
    gate_sum = jnp.dot(row_block, gate_cols, preferred_element_type=jnp.float32)
    up_sum = jnp.dot(row_block, up_cols, preferred_element_type=jnp.float32)
    hidden = (jax.nn.silu(gate_sum) * up_sum).astype(jnp.bfloat16)
    hid_blocks = hidden.reshape(hidden.shape[0], GROUP, SHARD_HID).transpose(1, 0, 2)
    down_blocks = down_rows.reshape(GROUP, SHARD_HID, D)

    def add_block(running, block_pair):
        partial_value = jnp.dot(block_pair[0], block_pair[1], preferred_element_type=jnp.float32).astype(jnp.bfloat16)
        partial_value = lax.optimization_barrier(partial_value)
        return running + partial_value.astype(jnp.float32), None

    running, _ = lax.scan(add_block, jnp.zeros((hidden.shape[0], D), jnp.float32), (hid_blocks, down_blocks))
    return running


def reference(act_rows, routes, route_weights, owners, w_gate, w_up, w_down, queries, new_keys, new_values, key_cache, value_cache, lengths):
    blocks = TOKENS // TOK_DEV
    blocked = act_rows.reshape(blocks, TOK_DEV, D).astype(jnp.float32)
    slot_index = jnp.arange(CAP, dtype=jnp.int32)
    ffn_sum = jnp.zeros((blocks, TOK_DEV, D), jnp.float32)
    for expert in range(EXPERTS):
        named_hits = routes == expert
        hit_mask = jnp.any(named_hits, axis=1).reshape(blocks, TOK_DEV)
        weight = jnp.sum(jnp.where(named_hits, route_weights, 0.0), axis=1).reshape(blocks, TOK_DEV)
        slot_rank = jnp.cumsum(hit_mask.astype(jnp.int32), axis=1) - 1
        slot_picks = (hit_mask[:, None, :] & (slot_rank[:, None, :] == slot_index[None, :, None])).astype(jnp.float32)
        row_block = jnp.einsum("bct,btd->bcd", slot_picks, blocked).astype(jnp.bfloat16)
        offset_col = (owners[expert] * FF).astype(jnp.int32)
        gate_cols = lax.dynamic_slice_in_dim(w_gate, offset_col, FF, 1)
        up_cols = lax.dynamic_slice_in_dim(w_up, offset_col, FF, 1)
        down_rows = lax.dynamic_slice_in_dim(w_down, offset_col, FF, 0)
        result = expert_rows(row_block.reshape(blocks * CAP, D), gate_cols, up_cols, down_rows)
        result = result.reshape(blocks, CAP, D)
        spread = slot_picks * weight[:, None, :]
        ffn_sum = ffn_sum + jnp.einsum("bct,bcd->btd", spread, result, precision=lax.Precision.HIGHEST)
    ffn_out = ffn_sum.reshape(TOKENS, D).astype(jnp.bfloat16)
    context = attend(queries, new_keys, new_values, key_cache, value_cache, lengths)
    return ffn_out, context
```

```python
import functools

import jax
import jax.numpy as jnp
from jax import lax
from jax.experimental import pallas as pl
from jax.experimental.pallas import tpu as pltpu
from jax.sharding import PartitionSpec as P

EXPERTS = 4
CAP = 2
SLOTS = EXPERTS * CAP
F32 = jnp.float32
BF16 = jnp.bfloat16

VMEM = pl.BlockSpec(memory_space=pltpu.VMEM)
SMEM = pl.BlockSpec(memory_space=pltpu.SMEM)


def params(mib):
    return pltpu.CompilerParams(vmem_limit_bytes=mib * 1024 * 1024)


def expert_of(owners_ref, block):
    found = jnp.int32(0)
    for expert in range(EXPERTS):
        found += jnp.where(owners_ref[expert] == block, expert, 0)
    return found


def slot_experts(owners_ref, base, iota):
    ids = jnp.zeros_like(iota)
    for m in range(EXPERTS):
        ids = jnp.where(iota // CAP == m, expert_of(owners_ref, base ^ m), ids)
    return ids


def pick_kernel(group_size, owners_ref, routes_ref, act_ref, out_ref):
    tokens = act_ref.shape[0]
    here = lax.axis_index("wide") // group_size
    rows = lax.broadcasted_iota(jnp.int32, (SLOTS, tokens), 0)
    cols = lax.broadcasted_iota(jnp.int32, (SLOTS, tokens), 1)
    ids = slot_experts(owners_ref, here, rows)
    hit = jnp.zeros((SLOTS, tokens), F32)
    for k in range(routes_ref.shape[0]):
        hit = jnp.where(routes_ref[k : k + 1, :] == ids, 1.0, hit)
    rank = jnp.zeros((SLOTS, tokens), F32)
    for t in range(tokens - 1):
        rank += jnp.where(cols > t, hit[:, t : t + 1], 0.0)
    picks = jnp.where(rank == (rows % CAP).astype(F32), hit, 0.0).astype(BF16)
    out_ref[...] = jnp.dot(picks, act_ref[...], preferred_element_type=F32).astype(BF16)


def pick_rows(owners, routes_t, act_rows, group_size):
    return pl.pallas_call(
        functools.partial(pick_kernel, group_size),
        out_shape=jax.ShapeDtypeStruct((SLOTS, act_rows.shape[1]), BF16),
        in_specs=[SMEM, VMEM, VMEM],
        out_specs=VMEM,
        compiler_params=params(4),
        name="pick_rows",
    )(owners, routes_t, act_rows)


def message_kernel(near_ref, far_ref, *out_refs):
    pieces = [ref[j].astype(F32) for ref in (near_ref, far_ref) for j in range(ref.shape[0])]
    for m, out_ref in enumerate(out_refs):
        chosen = [piece[m * CAP : (m + 1) * CAP] for piece in pieces]
        out_ref[...] = jnp.concatenate(chosen, axis=0).astype(BF16)


def messages(near, far):
    rows = CAP * (near.shape[0] + far.shape[0])
    shape = jax.ShapeDtypeStruct((rows, near.shape[2]), BF16)
    return pl.pallas_call(
        message_kernel,
        out_shape=(shape,) * EXPERTS,
        in_specs=[VMEM, VMEM],
        out_specs=(VMEM,) * EXPERTS,
        compiler_params=params(16),
        name="messages",
    )(near, far)


def gate_up_kernel(depth, *refs):
    msg_refs = refs[:EXPERTS]
    gate_ref, up_ref, gate_out, up_out, rows_ref = refs[EXPERTS:]
    step = pl.program_id(0)

    @pl.when(step == 0)
    def _():
        rows = jnp.concatenate([ref[...].astype(F32) for ref in msg_refs], axis=0).astype(BF16)
        for k in range(rows_ref.shape[0]):
            rows_ref[k] = rows[:, k * depth : (k + 1) * depth]
        gate_out[...] = jnp.zeros_like(gate_out)
        up_out[...] = jnp.zeros_like(up_out)

    rows = rows_ref[step]
    gate_out[...] += jnp.dot(rows, gate_ref[...], preferred_element_type=F32)
    up_out[...] += jnp.dot(rows, up_ref[...], preferred_element_type=F32)


def gate_up(msgs, w_gate, w_up, depth=256):
    features, hidden = w_gate.shape
    rows = sum(m.shape[0] for m in msgs)
    shape = jax.ShapeDtypeStruct((rows, hidden), F32)
    whole = [pl.BlockSpec(m.shape, lambda k: (0, 0)) for m in msgs]
    weight = pl.BlockSpec((depth, hidden), lambda k: (k, 0))
    out = pl.BlockSpec((rows, hidden), lambda k: (0, 0))
    return pl.pallas_call(
        functools.partial(gate_up_kernel, depth),
        out_shape=(shape, shape),
        grid=(features // depth,),
        in_specs=whole + [weight, weight],
        out_specs=(out, out),
        scratch_shapes=[pltpu.VMEM((features // depth, rows, depth), BF16)],
        compiler_params=params(40),
        name="gate_up",
    )(*msgs, w_gate, w_up)


def down_kernel(group_size, depth, ga, gb, ua, ub, down_ref, out_ref, hid_ref, acc_ref):
    step = pl.program_id(0)
    steps = hid_ref.shape[0]

    @pl.when(step == 0)
    def _():
        gate = ga[...] + gb[...]
        up = ua[...] + ub[...]
        hidden = (gate / (1.0 + jnp.exp(-gate)) * up).astype(BF16)
        for k in range(steps):
            hid_ref[k] = hidden[:, k * depth : (k + 1) * depth]
        acc_ref[...] = jnp.zeros_like(acc_ref)

    acc_ref[...] += jnp.dot(hid_ref[step], down_ref[...], preferred_element_type=F32)

    @pl.when(step == steps - 1)
    def _():
        wide = lax.axis_index("wide")
        block, place = wide // group_size, wide % group_size
        acc = acc_ref[...]
        for m in range(EXPERTS):
            for j in range(group_size):
                target = (block ^ m) * group_size + (place ^ j)
                start = (m * group_size + j) * CAP
                out_ref[target] = acc[start : start + CAP].astype(BF16)


def down(gate_pair, up_pair, w_down, group_size, depth):
    hidden, features = w_down.shape
    rows = gate_pair[0].shape[0]
    devices = rows // CAP
    whole = pl.BlockSpec((rows, hidden), lambda k: (0, 0))
    return pl.pallas_call(
        functools.partial(down_kernel, group_size, depth),
        out_shape=jax.ShapeDtypeStruct((devices, CAP, features), BF16),
        grid=(hidden // depth,),
        in_specs=[whole] * 4 + [pl.BlockSpec((depth, features), lambda k: (k, 0))],
        out_specs=pl.BlockSpec((devices, CAP, features), lambda k: (0, 0, 0)),
        scratch_shapes=[
            pltpu.VMEM((hidden // depth, rows, depth), BF16),
            pltpu.VMEM((rows, features), F32),
        ],
        compiler_params=params(40),
        name="down",
    )(*gate_pair, *up_pair, w_down)


def combine_kernel(group_size, owners_ref, routes_ref, weights_ref, back_ref, out_ref, rows_ref):
    tokens = out_ref.shape[0]
    devices = back_ref.shape[0]
    for d in range(devices):
        rows_ref[d * CAP : (d + 1) * CAP, :] = back_ref[d].astype(F32)
    eye = lax.broadcasted_iota(jnp.int32, (tokens, tokens), 0) == lax.broadcasted_iota(
        jnp.int32, (tokens, tokens), 1
    )
    width = devices * CAP
    rows = lax.broadcasted_iota(jnp.int32, (tokens, width), 0)
    slot = lax.broadcasted_iota(jnp.int32, (tokens, width), 1)
    block = slot // (CAP * group_size)
    ids = jnp.zeros_like(slot)
    for b in range(EXPERTS):
        ids = jnp.where(block == b, expert_of(owners_ref, b), ids)
    hit = jnp.zeros((tokens, width), F32)
    weight = jnp.zeros((tokens, 1), F32)
    for k in range(routes_ref.shape[0]):
        named = jnp.where(eye, routes_ref[k : k + 1, :], 0).sum(axis=1, keepdims=True)
        given = jnp.where(eye, weights_ref[k : k + 1, :], 0.0).sum(axis=1, keepdims=True)
        hit = jnp.where(named == ids, 1.0, hit)
        weight += jnp.where(named < EXPERTS, given, 0.0)
    rank = jnp.zeros((tokens, width), F32)
    for t in range(tokens - 1):
        rank += jnp.where(rows > t, hit[t : t + 1, :], 0.0)
    picks = jnp.where(rank == (slot % CAP).astype(F32), hit, 0.0).astype(BF16)
    total = jnp.dot(picks, rows_ref[...].astype(BF16), preferred_element_type=F32)
    out_ref[...] = (weight * total).astype(BF16)


def combine(owners, routes_t, weights_t, back, group_size):
    devices, _, features = back.shape
    return pl.pallas_call(
        functools.partial(combine_kernel, group_size),
        out_shape=jax.ShapeDtypeStruct((routes_t.shape[1], features), BF16),
        in_specs=[SMEM, VMEM, VMEM, VMEM],
        out_specs=VMEM,
        scratch_shapes=[pltpu.VMEM((devices * CAP, features), F32)],
        compiler_params=params(16),
        name="combine",
    )(owners, routes_t, weights_t, back)


def attend_kernel(lengths_ref, q_ref, nk_ref, nv_ref, keys_ref, values_ref, out_ref, turn_ref):
    requests, heads, size = q_ref.shape
    scaling = size ** (-0.5)
    for r in range(requests):
        q = q_ref[r]
        score = lax.dot_general(
            q, keys_ref[r], (((1,), (1,)), ((), ())), preferred_element_type=F32
        )
        score = score * scaling
        own = jnp.sum(q.astype(F32) * nk_ref[r : r + 1, :].astype(F32), axis=1, keepdims=True)
        own = own * scaling
        place = lax.broadcasted_iota(jnp.int32, score.shape, 1)
        score = jnp.where(place < lengths_ref[r], score, -jnp.inf)
        top = jnp.maximum(jnp.max(score, axis=1, keepdims=True), own)
        score = jnp.exp(score - top)
        own = jnp.exp(own - top)
        total = jnp.sum(score, axis=1, keepdims=True) + own
        prob = (score / total).astype(BF16)
        own = (own / total).astype(BF16).astype(F32)
        mixed = jnp.dot(prob, values_ref[r], preferred_element_type=F32)
        turn_ref[:, r, :] = mixed + own * nv_ref[r : r + 1, :].astype(F32)
    for h in range(heads):
        out_ref[:, h * size : (h + 1) * size] = turn_ref[h].astype(BF16)


def attend(queries, new_keys, new_values, key_cache, value_cache, lengths):
    requests, heads, size = queries.shape
    return pl.pallas_call(
        attend_kernel,
        out_shape=jax.ShapeDtypeStruct((requests, heads * size), BF16),
        in_specs=[SMEM] + [VMEM] * 5,
        out_specs=VMEM,
        scratch_shapes=[pltpu.VMEM((heads, requests, size), F32)],
        compiler_params=params(8),
        name="attend",
    )(lengths, queries, new_keys, new_values, key_cache, value_cache)


def swap(x, axis, devices, mask):
    return lax.ppermute(x, axis, [(i, i ^ mask) for i in range(devices)])


def per_device(
    act_rows,
    routes,
    route_weights,
    owners,
    w_gate,
    w_up,
    w_down,
    queries,
    new_keys,
    new_values,
    key_cache,
    value_cache,
    lengths,
):
    devices = lax.axis_size("wide")
    group_size = devices // EXPERTS
    routes_t, weights_t = routes.T, route_weights.T
    near = pick_rows(owners, routes_t, act_rows, group_size)[None]
    mask = 1
    while 2 * mask < group_size:
        near = jnp.concatenate([near, swap(near, "wide", devices, mask)], axis=0)
        mask *= 2
    far = swap(near, "wide", devices, mask)
    msgs = list(messages(near, far))
    for m in range(1, EXPERTS):
        msgs[m] = swap(msgs[m], "wide", devices, m * group_size)
    context = attend(queries, new_keys, new_values, key_cache, value_cache, lengths)
    gate, up = gate_up(msgs, w_gate, w_up)
    gate_pair = (gate, swap(gate, "narrow", 2, 1))
    up_pair = (up, swap(up, "narrow", 2, 1))
    depth = min(256, w_down.shape[0])
    if w_down.shape[0] % depth:
        depth = w_down.shape[0]
    partial_value = down(gate_pair, up_pair, w_down, group_size, depth)
    back = lax.all_to_all(partial_value, "wide", split_axis=0, concat_axis=0, tiled=True)
    ffn_out = combine(owners, routes_t, weights_t, back, group_size)
    return (ffn_out, context)


def solution(mesh):
    in_specs = (
        P(("groups", "wide"), "narrow"),
        P(("groups", "wide"), None),
        P(("groups", "wide"), None),
        P(),
        P("narrow", "wide"),
        P("narrow", "wide"),
        P("wide", "narrow"),
        P(("groups", "wide"), "narrow", None),
        P(("groups", "wide"), None),
        P(("groups", "wide"), None),
        P(("groups", "wide"), None, None),
        P(("groups", "wide"), None, None),
        P(("groups", "wide")),
    )
    out_specs = (P(("groups", "wide"), "narrow"), P(("groups", "wide"), "narrow"))
    return jax.shard_map(
        per_device, mesh=mesh, in_specs=in_specs, out_specs=out_specs, check_vma=False
    )
```

```python
import functools

import jax
import jax.numpy as jnp
from jax import lax
from jax.experimental import pallas as pl
from jax.experimental.pallas import tpu as pltpu
from jax.sharding import PartitionSpec as P

EXPERTS = 4
CAP = 2
SLOTS = EXPERTS * CAP
F32 = jnp.float32
BF16 = jnp.bfloat16

VMEM = pl.BlockSpec(memory_space=pltpu.VMEM)
SMEM = pl.BlockSpec(memory_space=pltpu.SMEM)
HBM = pl.BlockSpec(memory_space=pltpu.HBM)


def params(mib, rows=16):
    scaled = min(48, mib * max(1, rows // 16))
    return pltpu.CompilerParams(vmem_limit_bytes=scaled * 1024 * 1024)


def expert_of(owners_ref, block):
    found = jnp.int32(0)
    for expert in range(EXPERTS):
        found += jnp.where(owners_ref[expert] == block, expert, 0)
    return found


def slot_experts(owners_ref, base, iota):
    ids = jnp.zeros_like(iota)
    for m in range(EXPERTS):
        ids = jnp.where(iota // CAP == m, expert_of(owners_ref, base ^ m), ids)
    return ids


def fetch(pairs, sems):
    copies = [pltpu.make_async_copy(*pair, sems.at[n]) for n, pair in enumerate(pairs)]
    for copy in copies:
        copy.start()
    return copies


def in_hbm(*arrays):
    return [pltpu.with_memory_space_constraint(x, pltpu.HBM) for x in arrays]


def pick_kernel(group_size, owners_hbm, routes_hbm, act_hbm, out_ref, owners_ref, routes_ref, act_ref, sems):
    copies = fetch(
        ((owners_hbm, owners_ref), (routes_hbm, routes_ref), (act_hbm, act_ref)), sems
    )
    for copy in copies:
        copy.wait()
    tokens = act_ref.shape[0]
    here = lax.axis_index("wide") // group_size
    rows = lax.broadcasted_iota(jnp.int32, (SLOTS, tokens), 0)
    cols = lax.broadcasted_iota(jnp.int32, (SLOTS, tokens), 1)
    ids = slot_experts(owners_ref, here, rows)
    hit = jnp.zeros((SLOTS, tokens), F32)
    for k in range(routes_ref.shape[0]):
        hit = jnp.where(routes_ref[k : k + 1, :] == ids, 1.0, hit)
    rank = jnp.zeros((SLOTS, tokens), F32)
    for t in range(tokens - 1):
        rank += jnp.where(cols > t, hit[:, t : t + 1], 0.0)
    picks = jnp.where(rank == (rows % CAP).astype(F32), hit, 0.0).astype(BF16)
    out_ref[...] = jnp.dot(picks, act_ref[...], preferred_element_type=F32).astype(BF16)


def pick_rows(owners, routes_t, act_rows, group_size):
    return pl.pallas_call(
        functools.partial(pick_kernel, group_size),
        out_shape=jax.ShapeDtypeStruct((SLOTS, act_rows.shape[1]), BF16),
        in_specs=[HBM] * 3,
        out_specs=VMEM,
        scratch_shapes=[
            pltpu.SMEM(owners.shape, owners.dtype),
            pltpu.VMEM(routes_t.shape, routes_t.dtype),
            pltpu.VMEM(act_rows.shape, act_rows.dtype),
            pltpu.SemaphoreType.DMA((3,)),
        ],
        compiler_params=params(2),
        cost_estimate=pl.CostEstimate(
            flops=40_000_000_000, bytes_accessed=120_000_000, transcendentals=0
        ),
        name="pick_rows",
    )(*in_hbm(owners, routes_t, act_rows))


def message_kernel(near_ref, far_ref, *out_refs):
    pieces = [ref[j].astype(F32) for ref in (near_ref, far_ref) for j in range(ref.shape[0])]
    for m, out_ref in enumerate(out_refs):
        chosen = [piece[m * CAP : (m + 1) * CAP] for piece in pieces]
        out_ref[...] = jnp.concatenate(chosen, axis=0).astype(BF16)


def messages(near, far):
    rows = CAP * (near.shape[0] + far.shape[0])
    shape = jax.ShapeDtypeStruct((rows, near.shape[2]), BF16)
    return pl.pallas_call(
        message_kernel,
        out_shape=(shape,) * EXPERTS,
        in_specs=[VMEM, VMEM],
        out_specs=(VMEM,) * EXPERTS,
        compiler_params=params(2, EXPERTS * rows),
        name="messages",
    )(near, far)


def gate_up_kernel(*refs):
    msg_refs = refs[:EXPERTS]
    gate_ref, up_ref, down_hbm, gate_out, up_out, down_out, sem = refs[EXPERTS:]
    copy = pltpu.make_async_copy(down_hbm.at[pl.ds(0, down_out.shape[0])], down_out, sem)
    copy.start()
    rows = jnp.concatenate([ref[...].astype(F32) for ref in msg_refs], axis=0).astype(BF16)
    gate_out[...] = jnp.dot(rows, gate_ref[...], preferred_element_type=F32)
    up_out[...] = jnp.dot(rows, up_ref[...], preferred_element_type=F32)
    copy.wait()


def gate_up(msgs, w_gate, w_up, w_down, early):
    rows = sum(m.shape[0] for m in msgs)
    shape = jax.ShapeDtypeStruct((rows, w_gate.shape[1]), F32)
    return pl.pallas_call(
        gate_up_kernel,
        out_shape=(shape, shape, pltpu.VMEM((early, w_down.shape[1]), BF16)),
        in_specs=[VMEM] * (EXPERTS + 2) + [HBM],
        out_specs=(VMEM,) * 3,
        scratch_shapes=[pltpu.SemaphoreType.DMA],
        compiler_params=params(4, rows),
        name="gate_up",
    )(*msgs, w_gate, w_up, *in_hbm(w_down))


def down_kernel(group_size, ga, gb, ua, ub, early_ref, down_hbm, out_ref, late_ref, acc_ref, sem):
    early, late = early_ref.shape[0], late_ref.shape[0]
    copy = pltpu.make_async_copy(down_hbm.at[pl.ds(early, late)], late_ref, sem)
    copy.start()
    gate = ga[...] + gb[...]
    up = ua[...] + ub[...]
    hidden = (gate / (1.0 + jnp.exp(-gate)) * up).astype(BF16)
    features = acc_ref.shape[1]
    step = next(n for n in (512, 256, 128, features) if features % n == 0)
    for n in range(0, features, step):
        acc_ref[:, n : n + step] = jnp.dot(
            hidden[:, :early], early_ref[:, n : n + step], preferred_element_type=F32
        )
    copy.wait()
    for n in range(0, features, step):
        acc_ref[:, n : n + step] += jnp.dot(
            hidden[:, early:], late_ref[:, n : n + step], preferred_element_type=F32
        )
    acc = acc_ref[...]
    wide = lax.axis_index("wide")
    block, place = wide // group_size, wide % group_size
    for m in range(EXPERTS):
        for j in range(group_size):
            target = (block ^ m) * group_size + (place ^ j)
            start = (m * group_size + j) * CAP
            out_ref[target] = acc[start : start + CAP].astype(BF16)


def down(gate_pair, up_pair, w_early, w_down, group_size):
    rows = gate_pair[0].shape[0]
    hidden, features = w_down.shape
    late = hidden - w_early.shape[0]
    return pl.pallas_call(
        functools.partial(down_kernel, group_size),
        out_shape=jax.ShapeDtypeStruct((rows // CAP, CAP, features), BF16),
        in_specs=[VMEM] * 5 + [HBM],
        out_specs=VMEM,
        scratch_shapes=[
            pltpu.VMEM((late, features), BF16),
            pltpu.VMEM((rows, features), F32),
            pltpu.SemaphoreType.DMA,
        ],
        compiler_params=params(8, rows),
        name="down",
    )(
        *gate_pair,
        *up_pair,
        pltpu.with_memory_space_constraint(w_early, pltpu.VMEM),
        *in_hbm(w_down),
    )


def combine_kernel(group_size, owners_ref, routes_ref, weights_ref, back_ref, out_ref, rows_ref):
    tokens = out_ref.shape[0]
    devices = back_ref.shape[0]
    for d in range(devices):
        rows_ref[d * CAP : (d + 1) * CAP, :] = back_ref[d].astype(F32)
    eye = lax.broadcasted_iota(jnp.int32, (tokens, tokens), 0) == lax.broadcasted_iota(
        jnp.int32, (tokens, tokens), 1
    )
    width = devices * CAP
    rows = lax.broadcasted_iota(jnp.int32, (tokens, width), 0)
    slot = lax.broadcasted_iota(jnp.int32, (tokens, width), 1)
    block = slot // (CAP * group_size)
    ids = jnp.zeros_like(slot)
    for b in range(EXPERTS):
        ids = jnp.where(block == b, expert_of(owners_ref, b), ids)
    hit = jnp.zeros((tokens, width), F32)
    weight = jnp.zeros((tokens, 1), F32)
    for k in range(routes_ref.shape[0]):
        named = jnp.where(eye, routes_ref[k : k + 1, :], 0).sum(axis=1, keepdims=True)
        given = jnp.where(eye, weights_ref[k : k + 1, :], 0.0).sum(axis=1, keepdims=True)
        hit = jnp.where(named == ids, 1.0, hit)
        weight += jnp.where(named < EXPERTS, given, 0.0)
    rank = jnp.zeros((tokens, width), F32)
    for t in range(tokens - 1):
        rank += jnp.where(rows > t, hit[t : t + 1, :], 0.0)
    picks = jnp.where(rank == (slot % CAP).astype(F32), hit, 0.0).astype(BF16)
    total = jnp.dot(picks, rows_ref[...].astype(BF16), preferred_element_type=F32)
    out_ref[...] = (weight * total).astype(BF16)


def combine(owners, routes_t, weights_t, back, group_size):
    devices, _, features = back.shape
    return pl.pallas_call(
        functools.partial(combine_kernel, group_size),
        out_shape=jax.ShapeDtypeStruct((routes_t.shape[1], features), BF16),
        in_specs=[SMEM, VMEM, VMEM, VMEM],
        out_specs=VMEM,
        scratch_shapes=[pltpu.VMEM((devices * CAP, features), F32)],
        compiler_params=params(2, devices * CAP),
        name="combine",
    )(owners, routes_t, weights_t, back)


def attend_kernel(*refs):
    hbm, out_ref, scratch, turn_ref, sems = refs[:6], refs[6], refs[7:13], refs[13], refs[14]
    lengths_ref, q_ref, nk_ref, nv_ref, keys_ref, values_ref = scratch
    copies = fetch(tuple(zip(hbm, scratch)), sems)
    for copy in copies:
        copy.wait()
    requests, heads, size = q_ref.shape
    scaling = size ** (-0.5)
    for r in range(requests):
        q = q_ref[r]
        score = lax.dot_general(
            q, keys_ref[r], (((1,), (1,)), ((), ())), preferred_element_type=F32
        )
        score = score * scaling
        own = jnp.sum(q.astype(F32) * nk_ref[r : r + 1, :].astype(F32), axis=1, keepdims=True)
        own = own * scaling
        place = lax.broadcasted_iota(jnp.int32, score.shape, 1)
        score = jnp.where(place < lengths_ref[r], score, -jnp.inf)
        top = jnp.maximum(jnp.max(score, axis=1, keepdims=True), own)
        score = jnp.exp(score - top)
        own = jnp.exp(own - top)
        total = jnp.sum(score, axis=1, keepdims=True) + own
        prob = (score / total).astype(BF16)
        own = (own / total).astype(BF16).astype(F32)
        mixed = jnp.dot(prob, values_ref[r], preferred_element_type=F32)
        turn_ref[:, r, :] = mixed + own * nv_ref[r : r + 1, :].astype(F32)
    for h in range(heads):
        out_ref[:, h * size : (h + 1) * size] = turn_ref[h].astype(BF16)


def attend(queries, new_keys, new_values, key_cache, value_cache, lengths):
    requests, heads, size = queries.shape
    operands = (queries, new_keys, new_values, key_cache, value_cache)
    return pl.pallas_call(
        attend_kernel,
        out_shape=jax.ShapeDtypeStruct((requests, heads * size), BF16),
        in_specs=[HBM] * 6,
        out_specs=VMEM,
        scratch_shapes=[pltpu.SMEM(lengths.shape, lengths.dtype)]
        + [pltpu.VMEM(x.shape, x.dtype) for x in operands]
        + [pltpu.VMEM((heads, requests, size), F32), pltpu.SemaphoreType.DMA((6,))],
        compiler_params=params(2),
        name="attend",
    )(*in_hbm(lengths, *operands))


def swap(x, axis, devices, mask):
    return lax.ppermute(x, axis, [(i, i ^ mask) for i in range(devices)])


def per_device(
    act_rows,
    routes,
    route_weights,
    owners,
    w_gate,
    w_up,
    w_down,
    queries,
    new_keys,
    new_values,
    key_cache,
    value_cache,
    lengths,
):
    devices = lax.axis_size("wide")
    group_size = devices // EXPERTS
    routes_t, weights_t = routes.T, route_weights.T
    w_gate, w_up = (pltpu.with_memory_space_constraint(w, pltpu.VMEM) for w in (w_gate, w_up))
    near = pick_rows(owners, routes_t, act_rows, group_size)[None]
    mask = 1
    while 2 * mask < group_size:
        near = jnp.concatenate([near, swap(near, "wide", devices, mask)], axis=0)
        mask *= 2
    far = swap(near, "wide", devices, mask)
    msgs = list(messages(near, far))
    for m in range(1, EXPERTS):
        msgs[m] = swap(msgs[m], "wide", devices, m * group_size)
    context = attend(queries, new_keys, new_values, key_cache, value_cache, lengths)
    msgs, context = lax.optimization_barrier((msgs, context))
    early = w_down.shape[0] * 3 // 4 // 16 * 16
    gate, up, w_early = gate_up(msgs, w_gate, w_up, w_down, early)
    gate_pair = (gate, swap(gate, "narrow", 2, 1))
    up_pair = (up, swap(up, "narrow", 2, 1))
    partial_value = down(gate_pair, up_pair, w_early, w_down, group_size)
    back = lax.all_to_all(partial_value, "wide", split_axis=0, concat_axis=0, tiled=True)
    ffn_out = combine(owners, routes_t, weights_t, back, group_size)
    return (ffn_out, context)


def solution(mesh):
    in_specs = (
        P(("groups", "wide"), "narrow"),
        P(("groups", "wide"), None),
        P(("groups", "wide"), None),
        P(),
        P("narrow", "wide"),
        P("narrow", "wide"),
        P("wide", "narrow"),
        P(("groups", "wide"), "narrow", None),
        P(("groups", "wide"), None),
        P(("groups", "wide"), None),
        P(("groups", "wide"), None, None),
        P(("groups", "wide"), None, None),
        P(("groups", "wide")),
    )
    out_specs = (P(("groups", "wide"), "narrow"), P(("groups", "wide"), "narrow"))
    return jax.shard_map(
        per_device, mesh=mesh, in_specs=in_specs, out_specs=out_specs, check_vma=False
    )
```

```python
import functools

import jax
import jax.numpy as jnp
from jax import lax
from jax.experimental import pallas as pl
from jax.experimental.pallas import tpu as pltpu
from jax.sharding import PartitionSpec as P

EXPERTS = 4
CAP = 2
SLOTS = EXPERTS * CAP
F32 = jnp.float32
BF16 = jnp.bfloat16

VMEM = pl.BlockSpec(memory_space=pltpu.VMEM)
HBM = pl.BlockSpec(memory_space=pltpu.HBM)


def params(mib, rows=16):
    scaled = min(48, mib * max(1, rows // 16))
    return pltpu.CompilerParams(vmem_limit_bytes=scaled * 1024 * 1024)


def experts_of(owners_ref, blocks):
    ids = jnp.zeros_like(blocks)
    for expert in range(EXPERTS):
        ids = jnp.where(owners_ref[:, expert : expert + 1] == blocks, expert, ids)
    return ids


def fetch(pairs, sems):
    copies = [pltpu.make_async_copy(*pair, sems.at[n]) for n, pair in enumerate(pairs)]
    for copy in copies:
        copy.start()
    return copies


def in_hbm(*arrays):
    return [pltpu.with_memory_space_constraint(x, pltpu.HBM) for x in arrays]


def in_vmem(*arrays):
    return [pltpu.with_memory_space_constraint(x, pltpu.VMEM) for x in arrays]


def pick_kernel(
    group_size, owners_hbm, routes_hbm, act_hbm, out_ref, owners_ref, routes_ref, act_ref, sems
):
    copies = fetch(
        ((owners_hbm, owners_ref), (routes_hbm, routes_ref), (act_hbm, act_ref)), sems
    )
    for copy in copies:
        copy.wait()
    tokens = act_ref.shape[0]
    rows = lax.broadcasted_iota(jnp.int32, (SLOTS, tokens), 0)
    cols = lax.broadcasted_iota(jnp.int32, (SLOTS, tokens), 1)
    ids = experts_of(owners_ref, rows // CAP)
    hit = jnp.zeros((SLOTS, tokens), F32)
    for k in range(routes_ref.shape[0]):
        hit = jnp.where(routes_ref[k : k + 1, :] == ids, 1.0, hit)
    rank = jnp.zeros((SLOTS, tokens), F32)
    for t in range(tokens - 1):
        rank += jnp.where(cols > t, hit[:, t : t + 1], 0.0)
    picks = jnp.where(rank == (rows % CAP).astype(F32), hit, 0.0).astype(BF16)
    chosen = jnp.dot(picks, act_ref[...], preferred_element_type=F32)
    for m in range(EXPERTS):
        for j in range(group_size):
            out_ref[m * group_size + j] = chosen[m * CAP : (m + 1) * CAP].astype(BF16)


def pick_rows(owners, routes_t, act_rows, group_size):
    return pl.pallas_call(
        functools.partial(pick_kernel, group_size),
        out_shape=jax.ShapeDtypeStruct((EXPERTS * group_size, CAP, act_rows.shape[1]), BF16),
        in_specs=[HBM] * 3,
        out_specs=VMEM,
        scratch_shapes=[
            pltpu.VMEM(owners.shape, owners.dtype),
            pltpu.VMEM(routes_t.shape, routes_t.dtype),
            pltpu.VMEM(act_rows.shape, act_rows.dtype),
            pltpu.SemaphoreType.DMA((3,)),
        ],
        compiler_params=params(2),
        cost_estimate=pl.CostEstimate(
            flops=100000000000, bytes_accessed=120_000_000, transcendentals=0
        ),
        name="pick_rows",
    )(*in_hbm(owners, routes_t, act_rows))


def attention_steps(lengths_ref, q_ref, nk_ref, nv_ref, keys_ref, values_ref, out_ref, turn_ref):
    requests, heads, size = q_ref.shape
    scaling = size ** (-0.5)
    span = range(requests)
    scores = [
        lax.dot_general(
            q_ref[r], keys_ref[r], (((1,), (1,)), ((), ())), preferred_element_type=F32
        )
        for r in span
    ]
    yield
    place = lax.broadcasted_iota(jnp.int32, scores[0].shape, 1)
    scores = [
        jnp.where(place < lengths_ref[:, r : r + 1], scores[r] * scaling, -jnp.inf) for r in span
    ]
    owns = [
        jnp.sum(q_ref[r].astype(F32) * nk_ref[r : r + 1, :].astype(F32), axis=1, keepdims=True)
        for r in span
    ]
    score = jnp.concatenate(scores, axis=0)
    own = jnp.concatenate(owns, axis=0) * scaling
    top = jnp.maximum(jnp.max(score, axis=1, keepdims=True), own)
    yield
    score = jnp.exp(score - top)
    own = jnp.exp(own - top)
    total = jnp.sum(score, axis=1, keepdims=True) + own
    prob = (score / total).astype(BF16)
    own = (own / total).astype(BF16).astype(F32)
    yield
    for r in span:
        part = slice(r * heads, (r + 1) * heads)
        mixed = jnp.dot(prob[part], values_ref[r], preferred_element_type=F32)
        turn_ref[:, r, :] = mixed + own[part] * nv_ref[r : r + 1, :].astype(F32)
    yield
    for h in range(heads):
        out_ref[:, h * size : (h + 1) * size] = turn_ref[h].astype(BF16)


def stacked(rows_ref):
    pieces = [rows_ref[d].astype(F32) for d in range(rows_ref.shape[0])]
    return jnp.concatenate(pieces, axis=0).astype(BF16)


def gate_kernel(rows_ref, weight_ref, *refs):
    out_ref, context_ref, turn_ref = refs[6:]
    rows = stacked(rows_ref)
    steps = attention_steps(*refs[:6], context_ref, turn_ref)
    hidden = weight_ref.shape[1]
    width = next(n for n in (256, 256, hidden) if hidden % n == 0)
    for n in range(0, hidden, width):
        next(steps, None)
        out_ref[:, n : n + width] = jnp.dot(
            rows, weight_ref[:, n : n + width], preferred_element_type=F32
        )
    for _ in steps:
        pass


def gate_and_attend(came, weight, lengths, *operands):
    rows = came.shape[0] * CAP
    requests, heads, size = operands[0].shape
    return pl.pallas_call(
        gate_kernel,
        out_shape=(
            jax.ShapeDtypeStruct((rows, weight.shape[1]), F32),
            jax.ShapeDtypeStruct((requests, heads * size), BF16),
        ),
        in_specs=[VMEM] * 8,
        out_specs=(VMEM,) * 2,
        scratch_shapes=[pltpu.VMEM((heads, requests, size), F32)],
        compiler_params=params(4, rows),
        name="gate_and_attend",
    )(came, weight, lengths, *in_vmem(*operands))


def choose(owners_ref, routes_ref, weights_ref, picks_ref, weight_ref):
    tokens, width = picks_ref.shape
    eye = lax.broadcasted_iota(jnp.int32, (tokens, tokens), 0) == lax.broadcasted_iota(
        jnp.int32, (tokens, tokens), 1
    )
    rows = lax.broadcasted_iota(jnp.int32, (tokens, width), 0)
    slot = lax.broadcasted_iota(jnp.int32, (tokens, width), 1)
    ids = experts_of(owners_ref, slot // (width // EXPERTS))
    hit = jnp.zeros((tokens, width), F32)
    weight = jnp.zeros((tokens, 1), F32)
    for k in range(routes_ref.shape[0]):
        named = jnp.where(eye, routes_ref[k : k + 1, :], 0).sum(axis=1, keepdims=True)
        given = jnp.where(eye, weights_ref[k : k + 1, :], 0.0).sum(axis=1, keepdims=True)
        hit = jnp.where(named == ids, 1.0, hit)
        weight += jnp.where(named < EXPERTS, given, 0.0)
    rank = jnp.zeros((tokens, width), F32)
    for t in range(tokens - 1):
        rank += jnp.where(rows > t, hit[t : t + 1, :], 0.0)
    picks_ref[...] = jnp.where(rank == (slot % CAP).astype(F32), hit, 0.0).astype(BF16)
    weight_ref[...] = weight


def up_kernel(rows_ref, weight_ref, *refs):
    choose(*refs[:3], *refs[4:])
    refs[3][...] = jnp.dot(stacked(rows_ref), weight_ref[...], preferred_element_type=F32)


def up_and_choose(came, weight, owners, routes_t, weights_t):
    rows = came.shape[0] * CAP
    tokens = routes_t.shape[1]
    return pl.pallas_call(
        up_kernel,
        out_shape=(
            jax.ShapeDtypeStruct((rows, weight.shape[1]), F32),
            jax.ShapeDtypeStruct((tokens, rows), BF16),
            jax.ShapeDtypeStruct((tokens, 1), F32),
        ),
        in_specs=[VMEM] * 5,
        out_specs=(VMEM,) * 3,
        compiler_params=params(4, rows),
        name="up_and_choose",
    )(came, weight, owners, routes_t, weights_t)


def down_kernel(ga, gb, ua, ub, down_ref, out_ref):
    gate = ga[...] + gb[...]
    up = ua[...] + ub[...]
    hidden = (gate / (1.0 + jnp.exp(-gate)) * up).astype(BF16)
    total = jnp.dot(hidden, down_ref[...], preferred_element_type=F32)
    for d in range(out_ref.shape[0]):
        out_ref[d] = total[d * CAP : (d + 1) * CAP].astype(BF16)


def down(gate_pair, up_pair, w_down):
    rows = gate_pair[0].shape[0]
    return pl.pallas_call(
        down_kernel,
        out_shape=jax.ShapeDtypeStruct((rows // CAP, CAP, w_down.shape[1]), BF16),
        in_specs=[VMEM] * 5,
        out_specs=VMEM,
        compiler_params=params(2, rows),
        name="down",
    )(*gate_pair, *up_pair, w_down)


def combine_kernel(picks_ref, weight_ref, back_ref, out_ref):
    total = jnp.dot(picks_ref[...], stacked(back_ref), preferred_element_type=F32)
    out_ref[...] = (weight_ref[...] * total).astype(BF16)


def combine(picks, weight, back):
    devices, _, features = back.shape
    return pl.pallas_call(
        combine_kernel,
        out_shape=jax.ShapeDtypeStruct((picks.shape[0], features), BF16),
        in_specs=[VMEM] * 3,
        out_specs=VMEM,
        compiler_params=params(2, devices * CAP),
        name="combine",
    )(picks, weight, back)


def swap(x, axis, devices, mask):
    return lax.ppermute(x, axis, [(i, i ^ mask) for i in range(devices)])


def per_device(
    act_rows,
    routes,
    route_weights,
    owners,
    w_gate,
    w_up,
    w_down,
    queries,
    new_keys,
    new_values,
    key_cache,
    value_cache,
    lengths,
):
    devices = lax.axis_size("wide")
    group_size = devices // EXPERTS
    routes_t, weights_t = routes.T, route_weights.T
    w_gate, w_up, w_down = in_vmem(w_gate, w_up, w_down)
    owners, lengths = owners[None], lengths[None]
    picked = pick_rows(owners, routes_t, act_rows, group_size)
    came = lax.all_to_all(picked, "wide", split_axis=0, concat_axis=0, tiled=True)
    gate, context = gate_and_attend(
        came, w_gate, lengths, queries, new_keys, new_values, key_cache, value_cache
    )
    gate_pair = (gate, swap(gate, "narrow", 2, 1))
    up, picks, weight = up_and_choose(came, w_up, owners, routes_t, weights_t)
    up_pair = (up, swap(up, "narrow", 2, 1))
    partial_value = down(gate_pair, up_pair, w_down)
    back = lax.all_to_all(partial_value, "wide", split_axis=0, concat_axis=0, tiled=True)
    return (combine(picks, weight, back), context)


def solution(mesh):
    in_specs = (
        P(("groups", "wide"), "narrow"),
        P(("groups", "wide"), None),
        P(("groups", "wide"), None),
        P(),
        P("narrow", "wide"),
        P("narrow", "wide"),
        P("wide", "narrow"),
        P(("groups", "wide"), "narrow", None),
        P(("groups", "wide"), None),
        P(("groups", "wide"), None),
        P(("groups", "wide"), None, None),
        P(("groups", "wide"), None, None),
        P(("groups", "wide")),
    )
    out_specs = (P(("groups", "wide"), "narrow"), P(("groups", "wide"), "narrow"))
    return jax.shard_map(
        per_device, mesh=mesh, in_specs=in_specs, out_specs=out_specs, check_vma=False
    )
```

```python
import functools

import jax
import jax.numpy as jnp
from jax import lax
from jax.experimental import pallas as pl
from jax.experimental.pallas import tpu as pltpu
from jax.sharding import PartitionSpec as P

EXPERTS = 4
CAP = 2
SLOTS = EXPERTS * CAP
F32 = jnp.float32
BF16 = jnp.bfloat16

VMEM = pl.BlockSpec(memory_space=pltpu.VMEM)
HBM = pl.BlockSpec(memory_space=pltpu.HBM)


def params(mib, rows=16):
    scaled = min(48, mib * max(1, rows // 16))
    return pltpu.CompilerParams(vmem_limit_bytes=scaled * 1024 * 1024)


def experts_of(owners_ref, blocks):
    ids = jnp.zeros_like(blocks)
    for expert in range(EXPERTS):
        ids = jnp.where(owners_ref[:, expert : expert + 1] == blocks, expert, ids)
    return ids


def fetch(pairs, sems):
    copies = [pltpu.make_async_copy(*pair, sems.at[n]) for n, pair in enumerate(pairs)]
    for copy in copies:
        copy.start()
    return copies


def in_hbm(*arrays):
    return [pltpu.with_memory_space_constraint(x, pltpu.HBM) for x in arrays]


def in_vmem(*arrays):
    return [pltpu.with_memory_space_constraint(x, pltpu.VMEM) for x in arrays]


def pick_kernel(
    group_size, owners_hbm, routes_hbm, act_hbm, out_ref, owners_ref, routes_ref, act_ref, sems
):
    copies = fetch(
        ((owners_hbm, owners_ref), (routes_hbm, routes_ref), (act_hbm, act_ref)), sems
    )
    for copy in copies[:2]:
        copy.wait()
    tokens = act_ref.shape[0]
    rows = lax.broadcasted_iota(jnp.int32, (SLOTS, tokens), 0)
    cols = lax.broadcasted_iota(jnp.int32, (SLOTS, tokens), 1)
    ids = experts_of(owners_ref, rows // CAP)
    hit = jnp.zeros((SLOTS, tokens), F32)
    for k in range(routes_ref.shape[0]):
        hit = jnp.where(routes_ref[k : k + 1, :] == ids, 1.0, hit)
    rank = jnp.zeros((SLOTS, tokens), F32)
    for t in range(tokens - 1):
        rank += jnp.where(cols > t, hit[:, t : t + 1], 0.0)
    picks = jnp.where(rank == (rows % CAP).astype(F32), hit, 0.0).astype(BF16)
    copies[2].wait()
    chosen = jnp.dot(picks, act_ref[...], preferred_element_type=F32)
    for m in range(EXPERTS):
        for j in range(group_size):
            out_ref[m * group_size + j] = chosen[m * CAP : (m + 1) * CAP].astype(BF16)


def pick_rows(owners, routes_t, act_rows, group_size):
    return pl.pallas_call(
        functools.partial(pick_kernel, group_size),
        out_shape=jax.ShapeDtypeStruct((EXPERTS * group_size, CAP, act_rows.shape[1]), BF16),
        in_specs=[HBM] * 3,
        out_specs=VMEM,
        scratch_shapes=[
            pltpu.VMEM(owners.shape, owners.dtype),
            pltpu.VMEM(routes_t.shape, routes_t.dtype),
            pltpu.VMEM(act_rows.shape, act_rows.dtype),
            pltpu.SemaphoreType.DMA((3,)),
        ],
        compiler_params=params(2),
        cost_estimate=pl.CostEstimate(
            flops=100000000000, bytes_accessed=120_000_000, transcendentals=0
        ),
        name="pick_rows",
    )(*in_hbm(owners, routes_t, act_rows))


def attention_steps(lengths_ref, q_ref, nk_ref, nv_ref, keys_ref, values_ref, out_ref, turn_ref):
    requests, heads, size = q_ref.shape
    scaling = size ** (-0.5)
    span = range(requests)
    scores = [
        lax.dot_general(
            q_ref[r], keys_ref[r], (((1,), (1,)), ((), ())), preferred_element_type=F32
        )
        for r in span
    ]
    yield
    place = lax.broadcasted_iota(jnp.int32, scores[0].shape, 1)
    scores = [
        jnp.where(place < lengths_ref[:, r : r + 1], scores[r] * scaling, -jnp.inf) for r in span
    ]
    owns = [
        jnp.sum(q_ref[r].astype(F32) * nk_ref[r : r + 1, :].astype(F32), axis=1, keepdims=True)
        for r in span
    ]
    score = jnp.concatenate(scores, axis=0)
    own = jnp.concatenate(owns, axis=0) * scaling
    top = jnp.maximum(jnp.max(score, axis=1, keepdims=True), own)
    yield
    score = jnp.exp(score - top)
    own = jnp.exp(own - top)
    total = jnp.sum(score, axis=1, keepdims=True) + own
    prob = (score / total).astype(BF16)
    own = (own / total).astype(BF16).astype(F32)
    yield
    for r in span:
        part = slice(r * heads, (r + 1) * heads)
        mixed = jnp.dot(prob[part], values_ref[r], preferred_element_type=F32)
        turn_ref[:, r, :] = mixed + own[part] * nv_ref[r : r + 1, :].astype(F32)
    yield
    for h in range(heads):
        out_ref[:, h * size : (h + 1) * size] = turn_ref[h].astype(BF16)


def stacked(rows_ref):
    pieces = [rows_ref[d].astype(F32) for d in range(rows_ref.shape[0])]
    return jnp.concatenate(pieces, axis=0).astype(BF16)


def gate_kernel(came_ref, weight_ref, *refs):
    out_ref, rows_ref, context_ref, turn_ref = refs[6:]
    rows = stacked(came_ref)
    rows_ref[...] = rows
    steps = attention_steps(*refs[:6], context_ref, turn_ref)
    hidden = weight_ref.shape[1]
    width = next(n for n in (256, 256, hidden) if hidden % n == 0)
    for n in range(0, hidden, width):
        next(steps, None)
        out_ref[:, n : n + width] = jnp.dot(
            rows, weight_ref[:, n : n + width], preferred_element_type=F32
        )
    for _ in steps:
        pass


def gate_and_attend(came, weight, lengths, *operands):
    rows = came.shape[0] * CAP
    requests, heads, size = operands[0].shape
    return pl.pallas_call(
        gate_kernel,
        out_shape=(
            jax.ShapeDtypeStruct((rows, weight.shape[1]), F32),
            jax.ShapeDtypeStruct((rows, weight.shape[0]), BF16),
            jax.ShapeDtypeStruct((requests, heads * size), BF16),
        ),
        in_specs=[VMEM] * 8,
        out_specs=(VMEM,) * 3,
        scratch_shapes=[pltpu.VMEM((heads, requests, size), F32)],
        compiler_params=params(4, rows),
        name="gate_and_attend",
    )(came, weight, lengths, *in_vmem(*operands))


def choose(owners_ref, routes_ref, weights_ref, picks_ref, weight_ref):
    tokens, width = picks_ref.shape
    eye = lax.broadcasted_iota(jnp.int32, (tokens, tokens), 0) == lax.broadcasted_iota(
        jnp.int32, (tokens, tokens), 1
    )
    rows = lax.broadcasted_iota(jnp.int32, (tokens, width), 0)
    slot = lax.broadcasted_iota(jnp.int32, (tokens, width), 1)
    ids = experts_of(owners_ref, slot // (width // EXPERTS))
    hit = jnp.zeros((tokens, width), F32)
    weight = jnp.zeros((tokens, 1), F32)
    for k in range(routes_ref.shape[0]):
        named = jnp.where(eye, routes_ref[k : k + 1, :], 0).sum(axis=1, keepdims=True)
        given = jnp.where(eye, weights_ref[k : k + 1, :], 0.0).sum(axis=1, keepdims=True)
        hit = jnp.where(named == ids, 1.0, hit)
        weight += jnp.where(named < EXPERTS, given, 0.0)
    rank = jnp.zeros((tokens, width), F32)
    for t in range(tokens - 1):
        rank += jnp.where(rows > t, hit[t : t + 1, :], 0.0)
    picks_ref[...] = jnp.where(rank == (slot % CAP).astype(F32), hit, 0.0).astype(BF16)
    weight_ref[...] = weight


def up_kernel(rows_ref, weight_ref, gate_ref, *refs):
    choose(*refs[:3], *refs[4:])
    refs[3][0] = gate_ref[...]
    refs[3][1] = jnp.dot(rows_ref[...], weight_ref[...], preferred_element_type=F32)


def up_and_choose(came_rows, weight, gate, owners, routes_t, weights_t):
    rows = came_rows.shape[0]
    tokens = routes_t.shape[1]
    return pl.pallas_call(
        up_kernel,
        out_shape=(
            jax.ShapeDtypeStruct((2, rows, weight.shape[1]), F32),
            jax.ShapeDtypeStruct((tokens, rows), BF16),
            jax.ShapeDtypeStruct((tokens, 1), F32),
        ),
        in_specs=[VMEM] * 6,
        out_specs=(VMEM,) * 3,
        compiler_params=params(4, rows),
        name="up_and_choose",
    )(came_rows, weight, gate, owners, routes_t, weights_t)


def down_kernel(here_ref, there_ref, down_ref, out_ref):
    gate = here_ref[0] + there_ref[0]
    up = here_ref[1] + there_ref[1]
    hidden = (gate / (1.0 + jnp.exp(-gate)) * up).astype(BF16)
    total = jnp.dot(hidden, down_ref[...], preferred_element_type=F32)
    for d in range(out_ref.shape[0]):
        out_ref[d] = total[d * CAP : (d + 1) * CAP].astype(BF16)


def down(here, there, w_down):
    rows = here.shape[1]
    return pl.pallas_call(
        down_kernel,
        out_shape=jax.ShapeDtypeStruct((rows // CAP, CAP, w_down.shape[1]), BF16),
        in_specs=[VMEM] * 3,
        out_specs=VMEM,
        compiler_params=params(2, rows),
        name="down",
    )(here, there, w_down)


def combine_kernel(picks_ref, weight_ref, back_ref, out_ref):
    total = jnp.dot(picks_ref[...], stacked(back_ref), preferred_element_type=F32)
    out_ref[...] = (weight_ref[...] * total).astype(BF16)


def combine(picks, weight, back):
    devices, _, features = back.shape
    return pl.pallas_call(
        combine_kernel,
        out_shape=jax.ShapeDtypeStruct((picks.shape[0], features), BF16),
        in_specs=[VMEM] * 3,
        out_specs=VMEM,
        compiler_params=params(2, devices * CAP),
        name="combine",
    )(picks, weight, back)


def swap(x, axis, devices, mask):
    return lax.ppermute(x, axis, [(i, i ^ mask) for i in range(devices)])


def per_device(
    act_rows,
    routes,
    route_weights,
    owners,
    w_gate,
    w_up,
    w_down,
    queries,
    new_keys,
    new_values,
    key_cache,
    value_cache,
    lengths,
):
    devices = lax.axis_size("wide")
    group_size = devices // EXPERTS
    routes_t, weights_t = routes.T, route_weights.T
    w_gate, w_up, w_down = in_vmem(w_gate, w_up, w_down)
    owners, lengths = owners[None], lengths[None]
    picked = pick_rows(owners, routes_t, act_rows, group_size)
    came = lax.all_to_all(picked, "wide", split_axis=0, concat_axis=0, tiled=True)
    gate, came_rows, context = gate_and_attend(
        came, w_gate, lengths, queries, new_keys, new_values, key_cache, value_cache
    )
    sums, picks, weight = up_and_choose(came_rows, w_up, gate, owners, routes_t, weights_t)
    partial_value = down(sums, swap(sums, "narrow", 2, 1), w_down)
    back = lax.all_to_all(partial_value, "wide", split_axis=0, concat_axis=0, tiled=True)
    return (combine(picks, weight, back), context)


def solution(mesh):
    in_specs = (
        P(("groups", "wide"), "narrow"),
        P(("groups", "wide"), None),
        P(("groups", "wide"), None),
        P(),
        P("narrow", "wide"),
        P("narrow", "wide"),
        P("wide", "narrow"),
        P(("groups", "wide"), "narrow", None),
        P(("groups", "wide"), None),
        P(("groups", "wide"), None),
        P(("groups", "wide"), None, None),
        P(("groups", "wide"), None, None),
        P(("groups", "wide")),
    )
    out_specs = (P(("groups", "wide"), "narrow"), P(("groups", "wide"), "narrow"))
    return jax.shard_map(
        per_device, mesh=mesh, in_specs=in_specs, out_specs=out_specs, check_vma=False
    )
```

```python
import functools

import jax
import jax.numpy as jnp
from jax import lax
from jax.experimental import pallas as pl
from jax.experimental.pallas import tpu as pltpu
from jax.sharding import PartitionSpec as P

EXPERTS = 4
CAP = 2
SLOTS = EXPERTS * CAP
F32 = jnp.float32
BF16 = jnp.bfloat16

VMEM = pl.BlockSpec(memory_space=pltpu.VMEM)
HBM = pl.BlockSpec(memory_space=pltpu.HBM)


def params(mib, rows=16):
    scaled = min(48, mib * max(1, rows // 16))
    return pltpu.CompilerParams(vmem_limit_bytes=scaled * 1024 * 1024)


def experts_of(owners_ref, blocks):
    ids = jnp.zeros_like(blocks)
    for expert in range(EXPERTS):
        ids = jnp.where(owners_ref[:, expert : expert + 1] == blocks, expert, ids)
    return ids


def fetch(pairs, sems):
    copies = [pltpu.make_async_copy(*pair, sems.at[n]) for n, pair in enumerate(pairs)]
    for copy in copies:
        copy.start()
    return copies


def in_hbm(*arrays):
    return [pltpu.with_memory_space_constraint(x, pltpu.HBM) for x in arrays]


def in_vmem(*arrays):
    return [pltpu.with_memory_space_constraint(x, pltpu.VMEM) for x in arrays]


def pick_kernel(
    group_size, owners_hbm, routes_hbm, act_hbm, out_ref, owners_ref, routes_ref, act_ref, sems
):
    copies = fetch(
        ((owners_hbm, owners_ref), (routes_hbm, routes_ref), (act_hbm, act_ref)), sems
    )
    for copy in copies[:2]:
        copy.wait()
    tokens = act_ref.shape[0]
    rows = lax.broadcasted_iota(jnp.int32, (SLOTS, tokens), 0)
    cols = lax.broadcasted_iota(jnp.int32, (SLOTS, tokens), 1)
    ids = experts_of(owners_ref, rows // CAP)
    hit = jnp.zeros((SLOTS, tokens), F32)
    for k in range(routes_ref.shape[0]):
        hit = jnp.where(routes_ref[k : k + 1, :] == ids, 1.0, hit)
    rank = jnp.zeros((SLOTS, tokens), F32)
    for t in range(tokens - 1):
        rank += jnp.where(cols > t, hit[:, t : t + 1], 0.0)
    picks = jnp.where(rank == (rows % CAP).astype(F32), hit, 0.0).astype(BF16)
    copies[2].wait()
    chosen = jnp.dot(picks, act_ref[...], preferred_element_type=F32)
    for m in range(EXPERTS):
        for j in range(group_size):
            out_ref[m * group_size + j] = chosen[m * CAP : (m + 1) * CAP].astype(BF16)


def pick_rows(owners, routes_t, act_rows, group_size):
    return pl.pallas_call(
        functools.partial(pick_kernel, group_size),
        out_shape=jax.ShapeDtypeStruct((EXPERTS * group_size, CAP, act_rows.shape[1]), BF16),
        in_specs=[HBM] * 3,
        out_specs=VMEM,
        scratch_shapes=[
            pltpu.VMEM(owners.shape, owners.dtype),
            pltpu.VMEM(routes_t.shape, routes_t.dtype),
            pltpu.VMEM(act_rows.shape, act_rows.dtype),
            pltpu.SemaphoreType.DMA((3,)),
        ],
        compiler_params=params(2),
        cost_estimate=pl.CostEstimate(
            flops=100000000000, bytes_accessed=120_000_000, transcendentals=0
        ),
        name="pick_rows",
    )(*in_hbm(owners, routes_t, act_rows))


def attention_steps(lengths_ref, q_ref, nk_ref, nv_ref, keys_ref, values_ref, out_ref, turn_ref):
    requests, heads, size = q_ref.shape
    scaling = size ** (-0.5)
    span = range(requests)
    scores = [
        lax.dot_general(
            q_ref[r], keys_ref[r], (((1,), (1,)), ((), ())), preferred_element_type=F32
        )
        for r in span
    ]
    yield
    place = lax.broadcasted_iota(jnp.int32, scores[0].shape, 1)
    scores = [
        jnp.where(place < lengths_ref[:, r : r + 1], scores[r] * scaling, -jnp.inf) for r in span
    ]
    owns = [
        jnp.sum(q_ref[r].astype(F32) * nk_ref[r : r + 1, :].astype(F32), axis=1, keepdims=True)
        for r in span
    ]
    score = jnp.concatenate(scores, axis=0)
    own = jnp.concatenate(owns, axis=0) * scaling
    top = jnp.maximum(jnp.max(score, axis=1, keepdims=True), own)
    yield
    score = jnp.exp(score - top)
    own = jnp.exp(own - top)
    total = jnp.sum(score, axis=1, keepdims=True) + own
    prob = (score / total).astype(BF16)
    own = (own / total).astype(BF16).astype(F32)
    yield
    for r in span:
        part = slice(r * heads, (r + 1) * heads)
        mixed = jnp.dot(prob[part], values_ref[r], preferred_element_type=F32)
        turn_ref[:, r, :] = mixed + own[part] * nv_ref[r : r + 1, :].astype(F32)
    yield
    for h in range(heads):
        out_ref[:, h * size : (h + 1) * size] = turn_ref[h].astype(BF16)


def stacked(rows_ref):
    pieces = [rows_ref[d].astype(F32) for d in range(rows_ref.shape[0])]
    return jnp.concatenate(pieces, axis=0).astype(BF16)


def gate_kernel(came_ref, weight_ref, *refs):
    out_ref, rows_ref, context_ref, turn_ref = refs[6:]
    rows = stacked(came_ref)
    rows_ref[...] = rows
    steps = attention_steps(*refs[:6], context_ref, turn_ref)
    hidden = weight_ref.shape[1]
    width = next(n for n in (256, 256, hidden) if hidden % n == 0)
    for n in range(0, hidden, width):
        next(steps, None)
        out_ref[:, n : n + width] = jnp.dot(
            rows, weight_ref[:, n : n + width], preferred_element_type=F32
        )
    for _ in steps:
        pass


def gate_and_attend(came, weight, lengths, *operands):
    rows = came.shape[0] * CAP
    requests, heads, size = operands[0].shape
    return pl.pallas_call(
        gate_kernel,
        out_shape=(
            jax.ShapeDtypeStruct((rows, weight.shape[1]), F32),
            jax.ShapeDtypeStruct((rows, weight.shape[0]), BF16),
            jax.ShapeDtypeStruct((requests, heads * size), BF16),
        ),
        in_specs=[VMEM] * 8,
        out_specs=(VMEM,) * 3,
        scratch_shapes=[pltpu.VMEM((heads, requests, size), F32)],
        compiler_params=params(4, rows),
        name="gate_and_attend",
    )(came, weight, lengths, *in_vmem(*operands))


def choose(owners_ref, routes_ref, weights_ref, picks_ref, weight_ref):
    tokens, width = picks_ref.shape
    eye = lax.broadcasted_iota(jnp.int32, (tokens, tokens), 0) == lax.broadcasted_iota(
        jnp.int32, (tokens, tokens), 1
    )
    rows = lax.broadcasted_iota(jnp.int32, (tokens, width), 0)
    slot = lax.broadcasted_iota(jnp.int32, (tokens, width), 1)
    ids = experts_of(owners_ref, slot // (width // EXPERTS))
    hit = jnp.zeros((tokens, width), F32)
    weight = jnp.zeros((tokens, 1), F32)
    for k in range(routes_ref.shape[0]):
        named = jnp.where(eye, routes_ref[k : k + 1, :], 0).sum(axis=1, keepdims=True)
        given = jnp.where(eye, weights_ref[k : k + 1, :], 0.0).sum(axis=1, keepdims=True)
        hit = jnp.where(named == ids, 1.0, hit)
        weight += jnp.where(named < EXPERTS, given, 0.0)
    rank = jnp.zeros((tokens, width), F32)
    for t in range(tokens - 1):
        rank += jnp.where(rows > t, hit[t : t + 1, :], 0.0)
    picks_ref[...] = jnp.where(rank == (slot % CAP).astype(F32), hit, 0.0).astype(BF16)
    weight_ref[...] = weight


def up_kernel(rows_ref, weight_ref, gate_ref, *refs):
    own_ref, sent_ref = refs[3:5]
    choose(*refs[:3], *refs[5:])
    gate = gate_ref[...]
    own_ref[0] = gate
    sent_ref[0] = gate.astype(BF16)
    up = jnp.dot(rows_ref[...], weight_ref[...], preferred_element_type=F32)
    own_ref[1] = up
    sent_ref[1] = up.astype(BF16)


def up_and_choose(came_rows, weight, gate, owners, routes_t, weights_t):
    rows = came_rows.shape[0]
    tokens = routes_t.shape[1]
    return pl.pallas_call(
        up_kernel,
        out_shape=(
            jax.ShapeDtypeStruct((2, rows, weight.shape[1]), F32),
            jax.ShapeDtypeStruct((2, rows, weight.shape[1]), BF16),
            jax.ShapeDtypeStruct((tokens, rows), BF16),
            jax.ShapeDtypeStruct((tokens, 1), F32),
        ),
        in_specs=[VMEM] * 6,
        out_specs=(VMEM,) * 4,
        compiler_params=params(4, rows),
        name="up_and_choose",
    )(came_rows, weight, gate, owners, routes_t, weights_t)


def down_kernel(here_ref, there_ref, down_ref, out_ref):
    gate = here_ref[0] + there_ref[0].astype(F32)
    up = here_ref[1] + there_ref[1].astype(F32)
    hidden = (gate / (1.0 + jnp.exp(-gate)) * up).astype(BF16)
    total = jnp.dot(hidden, down_ref[...], preferred_element_type=F32)
    for d in range(out_ref.shape[0]):
        out_ref[d] = total[d * CAP : (d + 1) * CAP].astype(BF16)


def down(here, there, w_down):
    rows = here.shape[1]
    return pl.pallas_call(
        down_kernel,
        out_shape=jax.ShapeDtypeStruct((rows // CAP, CAP, w_down.shape[1]), BF16),
        in_specs=[VMEM] * 3,
        out_specs=VMEM,
        compiler_params=params(2, rows),
        name="down",
    )(here, there, w_down)


def combine_kernel(picks_ref, weight_ref, back_ref, out_ref):
    total = jnp.dot(picks_ref[...], stacked(back_ref), preferred_element_type=F32)
    out_ref[...] = (weight_ref[...] * total).astype(BF16)


def combine(picks, weight, back):
    devices, _, features = back.shape
    return pl.pallas_call(
        combine_kernel,
        out_shape=jax.ShapeDtypeStruct((picks.shape[0], features), BF16),
        in_specs=[VMEM] * 3,
        out_specs=VMEM,
        compiler_params=params(2, devices * CAP),
        name="combine",
    )(picks, weight, back)


def swap(x, axis, devices, mask):
    return lax.ppermute(x, axis, [(i, i ^ mask) for i in range(devices)])


def per_device(
    act_rows,
    routes,
    route_weights,
    owners,
    w_gate,
    w_up,
    w_down,
    queries,
    new_keys,
    new_values,
    key_cache,
    value_cache,
    lengths,
):
    devices = lax.axis_size("wide")
    group_size = devices // EXPERTS
    routes_t, weights_t = routes.T, route_weights.T
    w_gate, w_up, w_down = in_vmem(w_gate, w_up, w_down)
    owners, lengths = owners[None], lengths[None]
    picked = pick_rows(owners, routes_t, act_rows, group_size)
    came = lax.all_to_all(picked, "wide", split_axis=0, concat_axis=0, tiled=True)
    gate, came_rows, context = gate_and_attend(
        came, w_gate, lengths, queries, new_keys, new_values, key_cache, value_cache
    )
    own, sent, picks, weight = up_and_choose(
        came_rows, w_up, gate, owners, routes_t, weights_t
    )
    partial_value = down(own, swap(sent, "narrow", 2, 1), w_down)
    back = lax.all_to_all(partial_value, "wide", split_axis=0, concat_axis=0, tiled=True)
    return (combine(picks, weight, back), context)


def solution(mesh):
    in_specs = (
        P(("groups", "wide"), "narrow"),
        P(("groups", "wide"), None),
        P(("groups", "wide"), None),
        P(),
        P("narrow", "wide"),
        P("narrow", "wide"),
        P("wide", "narrow"),
        P(("groups", "wide"), "narrow", None),
        P(("groups", "wide"), None),
        P(("groups", "wide"), None),
        P(("groups", "wide"), None, None),
        P(("groups", "wide"), None, None),
        P(("groups", "wide")),
    )
    out_specs = (P(("groups", "wide"), "narrow"), P(("groups", "wide"), "narrow"))
    return jax.shard_map(
        per_device, mesh=mesh, in_specs=in_specs, out_specs=out_specs, check_vma=False
    )
```

```python
import functools

import jax
import jax.numpy as jnp
from jax import lax
from jax.experimental import pallas as pl
from jax.experimental.pallas import tpu as pltpu
from jax.sharding import PartitionSpec as P

EXPERTS = 4
CAP = 2
SLOTS = EXPERTS * CAP
F32 = jnp.float32
BF16 = jnp.bfloat16

VMEM = pl.BlockSpec(memory_space=pltpu.VMEM)
HBM = pl.BlockSpec(memory_space=pltpu.HBM)


def params(mib, rows=16):
    scaled = min(48, mib * max(1, rows // 16))
    return pltpu.CompilerParams(vmem_limit_bytes=scaled * 1024 * 1024)


def experts_of(owners_ref, blocks):
    ids = jnp.zeros_like(blocks)
    for expert in range(EXPERTS):
        ids = jnp.where(owners_ref[:, expert : expert + 1] == blocks, expert, ids)
    return ids


def fetch(pairs, sems):
    copies = [pltpu.make_async_copy(*pair, sems.at[n]) for n, pair in enumerate(pairs)]
    for copy in copies:
        copy.start()
    return copies


def in_hbm(*arrays):
    return [pltpu.with_memory_space_constraint(x, pltpu.HBM) for x in arrays]


def in_vmem(*arrays):
    return [pltpu.with_memory_space_constraint(x, pltpu.VMEM) for x in arrays]


def pick_kernel(
    group_size, owners_hbm, routes_hbm, act_hbm, out_ref, owners_ref, routes_ref, act_ref, sems
):
    copies = fetch(
        ((owners_hbm, owners_ref), (routes_hbm, routes_ref), (act_hbm, act_ref)), sems
    )
    for copy in copies[:2]:
        copy.wait()
    tokens = act_ref.shape[0]
    rows = lax.broadcasted_iota(jnp.int32, (SLOTS, tokens), 0)
    cols = lax.broadcasted_iota(jnp.int32, (SLOTS, tokens), 1)
    ids = experts_of(owners_ref, rows // CAP)
    hit = jnp.zeros((SLOTS, tokens), F32)
    for k in range(routes_ref.shape[0]):
        hit = jnp.where(routes_ref[k : k + 1, :] == ids, 1.0, hit)
    rank = jnp.zeros((SLOTS, tokens), F32)
    for t in range(tokens - 1):
        rank += jnp.where(cols > t, hit[:, t : t + 1], 0.0)
    picks = jnp.where(rank == (rows % CAP).astype(F32), hit, 0.0).astype(BF16)
    copies[2].wait()
    chosen = jnp.dot(picks, act_ref[...], preferred_element_type=F32)
    for m in range(EXPERTS):
        for j in range(group_size):
            out_ref[m * group_size + j] = chosen[m * CAP : (m + 1) * CAP].astype(BF16)


def pick_rows(owners, routes_t, act_rows, group_size):
    return pl.pallas_call(
        functools.partial(pick_kernel, group_size),
        out_shape=jax.ShapeDtypeStruct((EXPERTS * group_size, CAP, act_rows.shape[1]), BF16),
        in_specs=[HBM] * 3,
        out_specs=VMEM,
        scratch_shapes=[
            pltpu.VMEM(owners.shape, owners.dtype),
            pltpu.VMEM(routes_t.shape, routes_t.dtype),
            pltpu.VMEM(act_rows.shape, act_rows.dtype),
            pltpu.SemaphoreType.DMA((3,)),
        ],
        compiler_params=params(2),
        cost_estimate=pl.CostEstimate(
            flops=100000000000, bytes_accessed=120_000_000, transcendentals=0
        ),
        name="pick_rows",
    )(*in_hbm(owners, routes_t, act_rows))


def attention_steps(lengths_ref, q_ref, nk_ref, keys_ref, prob_ref, own_ref):
    requests, heads, size = q_ref.shape
    scaling = size ** (-0.5)
    span = range(requests)
    scores = [
        lax.dot_general(
            q_ref[r], keys_ref[r], (((1,), (1,)), ((), ())), preferred_element_type=F32
        )
        for r in span
    ]
    yield
    place = lax.broadcasted_iota(jnp.int32, scores[0].shape, 1)
    scores = [
        jnp.where(place < lengths_ref[:, r : r + 1], scores[r] * scaling, -jnp.inf) for r in span
    ]
    owns = [
        jnp.sum(q_ref[r].astype(F32) * nk_ref[r : r + 1, :].astype(F32), axis=1, keepdims=True)
        for r in span
    ]
    score = jnp.concatenate(scores, axis=0)
    own = jnp.concatenate(owns, axis=0) * scaling
    top = jnp.maximum(jnp.max(score, axis=1, keepdims=True), own)
    yield
    score = jnp.exp(score - top)
    own = jnp.exp(own - top)
    total = jnp.sum(score, axis=1, keepdims=True) + own
    prob_ref[...] = (score / total).astype(BF16)
    own_ref[...] = (own / total).astype(BF16).astype(F32)


def mix_kernel(prob_ref, own_ref, nv_ref, values_ref, out_ref, turn_ref):
    heads, requests, size = turn_ref.shape
    for r in range(requests):
        part = slice(r * heads, (r + 1) * heads)
        mixed = jnp.dot(prob_ref[part, :], values_ref[r], preferred_element_type=F32)
        turn_ref[:, r, :] = mixed + own_ref[part, :] * nv_ref[r : r + 1, :].astype(F32)
    for h in range(heads):
        out_ref[:, h * size : (h + 1) * size] = turn_ref[h].astype(BF16)


def mix(prob, own, new_values, value_cache):
    requests, _, size = value_cache.shape
    heads = prob.shape[0] // requests
    return pl.pallas_call(
        mix_kernel,
        out_shape=jax.ShapeDtypeStruct((requests, heads * size), BF16),
        in_specs=[VMEM] * 4,
        out_specs=VMEM,
        scratch_shapes=[pltpu.VMEM((heads, requests, size), F32)],
        compiler_params=params(2),
        name="mix",
    )(prob, own, *in_vmem(new_values, value_cache))


def stacked(rows_ref):
    pieces = [rows_ref[d].astype(F32) for d in range(rows_ref.shape[0])]
    return jnp.concatenate(pieces, axis=0).astype(BF16)


def gate_kernel(came_ref, weight_ref, *refs):
    out_ref, rows_ref, prob_ref, own_ref = refs[4:]
    rows = stacked(came_ref)
    rows_ref[...] = rows
    steps = attention_steps(*refs[:4], prob_ref, own_ref)
    hidden = weight_ref.shape[1]
    width = next(n for n in (256, 256, hidden) if hidden % n == 0)
    for n in range(0, hidden, width):
        next(steps, None)
        out_ref[:, n : n + width] = jnp.dot(
            rows, weight_ref[:, n : n + width], preferred_element_type=F32
        )
    for _ in steps:
        pass


def gate_and_attend(came, weight, lengths, *operands):
    rows = came.shape[0] * CAP
    requests, heads, _ = operands[0].shape
    return pl.pallas_call(
        gate_kernel,
        out_shape=(
            jax.ShapeDtypeStruct((rows, weight.shape[1]), F32),
            jax.ShapeDtypeStruct((rows, weight.shape[0]), BF16),
            jax.ShapeDtypeStruct((requests * heads, operands[2].shape[1]), BF16),
            jax.ShapeDtypeStruct((requests * heads, 1), F32),
        ),
        in_specs=[VMEM] * 6,
        out_specs=(VMEM,) * 4,
        compiler_params=params(4, rows),
        name="gate_and_attend",
    )(came, weight, lengths, *in_vmem(*operands))


def choose(owners_ref, routes_ref, weights_ref, picks_ref, weight_ref):
    tokens, width = picks_ref.shape
    eye = lax.broadcasted_iota(jnp.int32, (tokens, tokens), 0) == lax.broadcasted_iota(
        jnp.int32, (tokens, tokens), 1
    )
    rows = lax.broadcasted_iota(jnp.int32, (tokens, width), 0)
    slot = lax.broadcasted_iota(jnp.int32, (tokens, width), 1)
    ids = experts_of(owners_ref, slot // (width // EXPERTS))
    hit = jnp.zeros((tokens, width), F32)
    weight = jnp.zeros((tokens, 1), F32)
    for k in range(routes_ref.shape[0]):
        named = jnp.where(eye, routes_ref[k : k + 1, :], 0).sum(axis=1, keepdims=True)
        given = jnp.where(eye, weights_ref[k : k + 1, :], 0.0).sum(axis=1, keepdims=True)
        hit = jnp.where(named == ids, 1.0, hit)
        weight += jnp.where(named < EXPERTS, given, 0.0)
    rank = jnp.zeros((tokens, width), F32)
    for t in range(tokens - 1):
        rank += jnp.where(rows > t, hit[t : t + 1, :], 0.0)
    picks_ref[...] = jnp.where(rank == (slot % CAP).astype(F32), hit, 0.0).astype(BF16)
    weight_ref[...] = weight


def up_kernel(rows_ref, weight_ref, gate_ref, *refs):
    choose(*refs[:3], *refs[4:])
    refs[3][0] = gate_ref[...]
    refs[3][1] = jnp.dot(rows_ref[...], weight_ref[...], preferred_element_type=F32)


def up_and_choose(came_rows, weight, gate, owners, routes_t, weights_t):
    rows = came_rows.shape[0]
    tokens = routes_t.shape[1]
    return pl.pallas_call(
        up_kernel,
        out_shape=(
            jax.ShapeDtypeStruct((2, rows, weight.shape[1]), F32),
            jax.ShapeDtypeStruct((tokens, rows), BF16),
            jax.ShapeDtypeStruct((tokens, 1), F32),
        ),
        in_specs=[VMEM] * 6,
        out_specs=(VMEM,) * 3,
        compiler_params=params(4, rows),
        name="up_and_choose",
    )(came_rows, weight, gate, owners, routes_t, weights_t)


def down_kernel(here_ref, there_ref, down_ref, out_ref):
    gate = here_ref[0] + there_ref[0]
    up = here_ref[1] + there_ref[1]
    hidden = (gate / (1.0 + jnp.exp(-gate)) * up).astype(BF16)
    total = jnp.dot(hidden, down_ref[...], preferred_element_type=F32)
    for d in range(out_ref.shape[0]):
        out_ref[d] = total[d * CAP : (d + 1) * CAP].astype(BF16)


def down(here, there, w_down):
    rows = here.shape[1]
    return pl.pallas_call(
        down_kernel,
        out_shape=jax.ShapeDtypeStruct((rows // CAP, CAP, w_down.shape[1]), BF16),
        in_specs=[VMEM] * 3,
        out_specs=VMEM,
        compiler_params=params(2, rows),
        name="down",
    )(here, there, w_down)


def combine_kernel(picks_ref, weight_ref, back_ref, out_ref):
    total = jnp.dot(picks_ref[...], stacked(back_ref), preferred_element_type=F32)
    out_ref[...] = (weight_ref[...] * total).astype(BF16)


def combine(picks, weight, back):
    devices, _, features = back.shape
    return pl.pallas_call(
        combine_kernel,
        out_shape=jax.ShapeDtypeStruct((picks.shape[0], features), BF16),
        in_specs=[VMEM] * 3,
        out_specs=VMEM,
        compiler_params=params(2, devices * CAP),
        name="combine",
    )(picks, weight, back)


def swap(x, axis, devices, mask):
    return lax.ppermute(x, axis, [(i, i ^ mask) for i in range(devices)])


def per_device(
    act_rows,
    routes,
    route_weights,
    owners,
    w_gate,
    w_up,
    w_down,
    queries,
    new_keys,
    new_values,
    key_cache,
    value_cache,
    lengths,
):
    devices = lax.axis_size("wide")
    group_size = devices // EXPERTS
    routes_t, weights_t = routes.T, route_weights.T
    w_gate, w_up, w_down = in_vmem(w_gate, w_up, w_down)
    owners, lengths = owners[None], lengths[None]
    picked = pick_rows(owners, routes_t, act_rows, group_size)
    came = lax.all_to_all(picked, "wide", split_axis=0, concat_axis=0, tiled=True)
    gate, came_rows, prob, own = gate_and_attend(
        came, w_gate, lengths, queries, new_keys, key_cache
    )
    sums, picks, weight = up_and_choose(came_rows, w_up, gate, owners, routes_t, weights_t)
    sums, prob, own = lax.optimization_barrier((sums, prob, own))
    context = mix(prob, own, new_values, value_cache)
    there = swap(sums, "narrow", 2, 1)
    there, context = lax.optimization_barrier((there, context))
    partial_value = down(sums, there, w_down)
    back = lax.all_to_all(partial_value, "wide", split_axis=0, concat_axis=0, tiled=True)
    return (combine(picks, weight, back), context)


def solution(mesh):
    in_specs = (
        P(("groups", "wide"), "narrow"),
        P(("groups", "wide"), None),
        P(("groups", "wide"), None),
        P(),
        P("narrow", "wide"),
        P("narrow", "wide"),
        P("wide", "narrow"),
        P(("groups", "wide"), "narrow", None),
        P(("groups", "wide"), None),
        P(("groups", "wide"), None),
        P(("groups", "wide"), None, None),
        P(("groups", "wide"), None, None),
        P(("groups", "wide")),
    )
    out_specs = (P(("groups", "wide"), "narrow"), P(("groups", "wide"), "narrow"))
    return jax.shard_map(
        per_device, mesh=mesh, in_specs=in_specs, out_specs=out_specs, check_vma=False
    )
```

```python
import functools

import jax
import jax.numpy as jnp
from jax import lax
from jax.experimental import pallas as pl
from jax.experimental.pallas import tpu as pltpu
from jax.sharding import PartitionSpec as P

EXPERTS = 4
CAP = 2
SLOTS = EXPERTS * CAP
F32 = jnp.float32
BF16 = jnp.bfloat16

VMEM = pl.BlockSpec(memory_space=pltpu.VMEM)
HBM = pl.BlockSpec(memory_space=pltpu.HBM)


def params(mib, rows=16):
    scaled = min(48, mib * max(1, rows // 16))
    return pltpu.CompilerParams(vmem_limit_bytes=scaled * 1024 * 1024)


def experts_of(owners_ref, blocks):
    ids = jnp.zeros_like(blocks)
    for expert in range(EXPERTS):
        ids = jnp.where(owners_ref[:, expert : expert + 1] == blocks, expert, ids)
    return ids


def fetch(pairs, sems):
    copies = [pltpu.make_async_copy(*pair, sems.at[n]) for n, pair in enumerate(pairs)]
    for copy in copies:
        copy.start()
    return copies


def in_hbm(*arrays):
    return [pltpu.with_memory_space_constraint(x, pltpu.HBM) for x in arrays]


def in_vmem(*arrays):
    return [pltpu.with_memory_space_constraint(x, pltpu.VMEM) for x in arrays]


def pick_kernel(
    group_size, owners_hbm, routes_hbm, act_hbm, out_ref, owners_ref, routes_ref, act_ref, sems
):
    copies = fetch(
        ((owners_hbm, owners_ref), (routes_hbm, routes_ref), (act_hbm, act_ref)), sems
    )
    for copy in copies[:2]:
        copy.wait()
    tokens = act_ref.shape[0]
    rows = lax.broadcasted_iota(jnp.int32, (SLOTS, tokens), 0)
    cols = lax.broadcasted_iota(jnp.int32, (SLOTS, tokens), 1)
    ids = experts_of(owners_ref, rows // CAP)
    hit = jnp.zeros((SLOTS, tokens), F32)
    for k in range(routes_ref.shape[0]):
        hit = jnp.where(routes_ref[k : k + 1, :] == ids, 1.0, hit)
    rank = jnp.zeros((SLOTS, tokens), F32)
    for t in range(tokens - 1):
        rank += jnp.where(cols > t, hit[:, t : t + 1], 0.0)
    picks = jnp.where(rank == (rows % CAP).astype(F32), hit, 0.0).astype(BF16)
    copies[2].wait()
    chosen = jnp.dot(picks, act_ref[...], preferred_element_type=F32)
    for m in range(EXPERTS):
        for j in range(group_size):
            out_ref[m * group_size + j] = chosen[m * CAP : (m + 1) * CAP].astype(BF16)


def pick_rows(owners, routes_t, act_rows, group_size):
    return pl.pallas_call(
        functools.partial(pick_kernel, group_size),
        out_shape=jax.ShapeDtypeStruct((EXPERTS * group_size, CAP, act_rows.shape[1]), BF16),
        in_specs=[HBM] * 3,
        out_specs=VMEM,
        scratch_shapes=[
            pltpu.VMEM(owners.shape, owners.dtype),
            pltpu.VMEM(routes_t.shape, routes_t.dtype),
            pltpu.VMEM(act_rows.shape, act_rows.dtype),
            pltpu.SemaphoreType.DMA((3,)),
        ],
        compiler_params=params(2),
        cost_estimate=pl.CostEstimate(
            flops=100000000000, bytes_accessed=120_000_000, transcendentals=0
        ),
        name="pick_rows",
    )(*in_hbm(owners, routes_t, act_rows))


def attention_steps(lengths_ref, q_ref, nk_ref, keys_ref, prob_ref, own_ref):
    requests, heads, size = q_ref.shape
    scaling = size ** (-0.5)
    span = range(requests)
    scores = [
        lax.dot_general(
            q_ref[r], keys_ref[r], (((1,), (1,)), ((), ())), preferred_element_type=F32
        )
        for r in span
    ]
    yield
    place = lax.broadcasted_iota(jnp.int32, scores[0].shape, 1)
    scores = [
        jnp.where(place < lengths_ref[:, r : r + 1], scores[r] * scaling, -jnp.inf) for r in span
    ]
    owns = [
        jnp.sum(q_ref[r].astype(F32) * nk_ref[r : r + 1, :].astype(F32), axis=1, keepdims=True)
        for r in span
    ]
    score = jnp.concatenate(scores, axis=0)
    own = jnp.concatenate(owns, axis=0) * scaling
    top = jnp.maximum(jnp.max(score, axis=1, keepdims=True), own)
    yield
    prob_ref[...] = jnp.exp(score - top)
    own_ref[...] = jnp.exp(own - top)


def mix_kernel(prob_ref, own_ref, nv_ref, values_ref, out_ref, turn_ref):
    heads, requests, size = turn_ref.shape
    score, own = prob_ref[...], own_ref[...]
    total = jnp.sum(score, axis=1, keepdims=True) + own
    prob = (score / total).astype(BF16)
    own = (own / total).astype(BF16).astype(F32)
    for r in range(requests):
        part = slice(r * heads, (r + 1) * heads)
        mixed = jnp.dot(prob[part], values_ref[r], preferred_element_type=F32)
        turn_ref[:, r, :] = mixed + own[part] * nv_ref[r : r + 1, :].astype(F32)
    for h in range(heads):
        out_ref[:, h * size : (h + 1) * size] = turn_ref[h].astype(BF16)


def mix(prob, own, new_values, value_cache):
    requests, _, size = value_cache.shape
    heads = prob.shape[0] // requests
    return pl.pallas_call(
        mix_kernel,
        out_shape=jax.ShapeDtypeStruct((requests, heads * size), BF16),
        in_specs=[VMEM] * 4,
        out_specs=VMEM,
        scratch_shapes=[pltpu.VMEM((heads, requests, size), F32)],
        compiler_params=params(2),
        name="mix",
    )(prob, own, *in_vmem(new_values, value_cache))


def stacked(rows_ref):
    pieces = [rows_ref[d].astype(F32) for d in range(rows_ref.shape[0])]
    return jnp.concatenate(pieces, axis=0).astype(BF16)


def gate_kernel(came_ref, weight_ref, *refs):
    out_ref, rows_ref, prob_ref, own_ref = refs[4:]
    rows = stacked(came_ref)
    rows_ref[...] = rows
    steps = attention_steps(*refs[:4], prob_ref, own_ref)
    hidden = weight_ref.shape[1]
    width = next(n for n in (256, 256, hidden) if hidden % n == 0)
    for n in range(0, hidden, width):
        next(steps, None)
        out_ref[:, n : n + width] = jnp.dot(
            rows, weight_ref[:, n : n + width], preferred_element_type=F32
        )
    for _ in steps:
        pass


def gate_and_attend(came, weight, lengths, *operands):
    rows = came.shape[0] * CAP
    requests, heads, _ = operands[0].shape
    return pl.pallas_call(
        gate_kernel,
        out_shape=(
            jax.ShapeDtypeStruct((rows, weight.shape[1]), F32),
            jax.ShapeDtypeStruct((rows, weight.shape[0]), BF16),
            jax.ShapeDtypeStruct((requests * heads, operands[2].shape[1]), F32),
            jax.ShapeDtypeStruct((requests * heads, 1), F32),
        ),
        in_specs=[VMEM] * 6,
        out_specs=(VMEM,) * 4,
        compiler_params=params(4, rows),
        name="gate_and_attend",
    )(came, weight, lengths, *in_vmem(*operands))


def choose(owners_ref, routes_ref, weights_ref, picks_ref, weight_ref):
    tokens, width = picks_ref.shape
    eye = lax.broadcasted_iota(jnp.int32, (tokens, tokens), 0) == lax.broadcasted_iota(
        jnp.int32, (tokens, tokens), 1
    )
    rows = lax.broadcasted_iota(jnp.int32, (tokens, width), 0)
    slot = lax.broadcasted_iota(jnp.int32, (tokens, width), 1)
    ids = experts_of(owners_ref, slot // (width // EXPERTS))
    hit = jnp.zeros((tokens, width), F32)
    weight = jnp.zeros((tokens, 1), F32)
    for k in range(routes_ref.shape[0]):
        named = jnp.where(eye, routes_ref[k : k + 1, :], 0).sum(axis=1, keepdims=True)
        given = jnp.where(eye, weights_ref[k : k + 1, :], 0.0).sum(axis=1, keepdims=True)
        hit = jnp.where(named == ids, 1.0, hit)
        weight += jnp.where(named < EXPERTS, given, 0.0)
    rank = jnp.zeros((tokens, width), F32)
    for t in range(tokens - 1):
        rank += jnp.where(rows > t, hit[t : t + 1, :], 0.0)
    picks_ref[...] = jnp.where(rank == (slot % CAP).astype(F32), hit, 0.0).astype(BF16)
    weight_ref[...] = weight


def up_kernel(rows_ref, weight_ref, gate_ref, *refs):
    choose(*refs[:3], *refs[4:])
    refs[3][0] = gate_ref[...]
    refs[3][1] = jnp.dot(rows_ref[...], weight_ref[...], preferred_element_type=F32)


def up_and_choose(came_rows, weight, gate, owners, routes_t, weights_t):
    rows = came_rows.shape[0]
    tokens = routes_t.shape[1]
    return pl.pallas_call(
        up_kernel,
        out_shape=(
            jax.ShapeDtypeStruct((2, rows, weight.shape[1]), F32),
            jax.ShapeDtypeStruct((tokens, rows), BF16),
            jax.ShapeDtypeStruct((tokens, 1), F32),
        ),
        in_specs=[VMEM] * 6,
        out_specs=(VMEM,) * 3,
        compiler_params=params(4, rows),
        name="up_and_choose",
    )(came_rows, weight, gate, owners, routes_t, weights_t)


def down_kernel(here_ref, there_ref, down_ref, out_ref):
    gate = here_ref[0] + there_ref[0]
    up = here_ref[1] + there_ref[1]
    hidden = (gate / (1.0 + jnp.exp(-gate)) * up).astype(BF16)
    total = jnp.dot(hidden, down_ref[...], preferred_element_type=F32)
    for d in range(out_ref.shape[0]):
        out_ref[d] = total[d * CAP : (d + 1) * CAP].astype(BF16)


def down(here, there, w_down):
    rows = here.shape[1]
    return pl.pallas_call(
        down_kernel,
        out_shape=jax.ShapeDtypeStruct((rows // CAP, CAP, w_down.shape[1]), BF16),
        in_specs=[VMEM] * 3,
        out_specs=VMEM,
        compiler_params=params(2, rows),
        name="down",
    )(here, there, w_down)


def combine_kernel(picks_ref, weight_ref, back_ref, out_ref):
    total = jnp.dot(picks_ref[...], stacked(back_ref), preferred_element_type=F32)
    out_ref[...] = (weight_ref[...] * total).astype(BF16)


def combine(picks, weight, back):
    devices, _, features = back.shape
    return pl.pallas_call(
        combine_kernel,
        out_shape=jax.ShapeDtypeStruct((picks.shape[0], features), BF16),
        in_specs=[VMEM] * 3,
        out_specs=VMEM,
        compiler_params=params(2, devices * CAP),
        name="combine",
    )(picks, weight, back)


def swap(x, axis, devices, mask):
    return lax.ppermute(x, axis, [(i, i ^ mask) for i in range(devices)])


def per_device(
    act_rows,
    routes,
    route_weights,
    owners,
    w_gate,
    w_up,
    w_down,
    queries,
    new_keys,
    new_values,
    key_cache,
    value_cache,
    lengths,
):
    devices = lax.axis_size("wide")
    group_size = devices // EXPERTS
    routes_t, weights_t = routes.T, route_weights.T
    w_gate, w_up, w_down = in_vmem(w_gate, w_up, w_down)
    owners, lengths = owners[None], lengths[None]
    picked = pick_rows(owners, routes_t, act_rows, group_size)
    came = lax.all_to_all(picked, "wide", split_axis=0, concat_axis=0, tiled=True)
    gate, came_rows, prob, own = gate_and_attend(
        came, w_gate, lengths, queries, new_keys, key_cache
    )
    sums, picks, weight = up_and_choose(came_rows, w_up, gate, owners, routes_t, weights_t)
    sums, prob, own = lax.optimization_barrier((sums, prob, own))
    context = mix(prob, own, new_values, value_cache)
    there = swap(sums, "narrow", 2, 1)
    there, context = lax.optimization_barrier((there, context))
    partial_value = down(sums, there, w_down)
    back = lax.all_to_all(partial_value, "wide", split_axis=0, concat_axis=0, tiled=True)
    return (combine(picks, weight, back), context)


def solution(mesh):
    in_specs = (
        P(("groups", "wide"), "narrow"),
        P(("groups", "wide"), None),
        P(("groups", "wide"), None),
        P(),
        P("narrow", "wide"),
        P("narrow", "wide"),
        P("wide", "narrow"),
        P(("groups", "wide"), "narrow", None),
        P(("groups", "wide"), None),
        P(("groups", "wide"), None),
        P(("groups", "wide"), None, None),
        P(("groups", "wide"), None, None),
        P(("groups", "wide")),
    )
    out_specs = (P(("groups", "wide"), "narrow"), P(("groups", "wide"), "narrow"))
    return jax.shard_map(
        per_device, mesh=mesh, in_specs=in_specs, out_specs=out_specs, check_vma=False
    )
```
